32 devices in a mesh: ctx: 4 (over x, core), tp: 8 (over z, y).
Axes of the slice: x: 2, y: 2, z: 4, core: 2. Of those that a mesh axis runs over, the one named last changes fastest.
Arguments:
- residual: bfloat16 [1024, 8192], P('ctx', 'tp'), may hold values from -8 to 8
- queries: bfloat16 [1024, 8192], P('ctx', 'tp'), may hold values from -15 to 15
- keys_values: bfloat16 [1024, 2048], P('ctx'), may hold values from -6 to 6
- out_weight: bfloat16 [8192, 8192], P('tp', 'ctx'), may hold values from -0.09375 to 0.09375
- norm_gain: float32 [8192], replicated, may hold values from 0.1 to 1.9
- cache_weight: bfloat16 [8192, 2048], P(None, 'tp'), may hold values from -0.0625 to 0.0625
- positions: int32 [1024], P('ctx'), may hold values from 0 to 2047, as said below
- keep_rows: int32 [1024], P('ctx'), may hold values from 0 to 255, as said below
- kept_count: int32 [4], P('ctx'), may hold values from 64 to 256, as said below
Outputs:
- kept_hidden: bfloat16 [1024, 8192], P('ctx', 'tp')
- kept_cache: bfloat16 [1024, 2048], P('ctx', 'tp')
The draws below stay inside these ranges and needn't reach their ends.
Inputs may be any that keep to these rules, and one draw needn't show every extreme that they name: `keep_rows`: within every shard of ctx the 256 entries are a permutation of the shard's local rows: first its kept rows in ascending order, as many as its kept_count, then its dropped rows in ascending order. `kept_count`: for every even shard index e, shards e and e + 1 keep 2 * 160 rows together. `positions`: strictly increasing along the tokens.
All inputs are finite; a program needn't handle non-finite values.
Results may differ from the reference program's by a relative error of at most 0.019.
Values may be sent and summed in bfloat16 or wider, within the bound.
A program may use at most 64 MiB of HBM per device.

```python
import math
import jax
import jax.numpy as jnp
from jax import lax

D = 8192
HQ = 64
KVH = 8
HD = 128
TOK_DEV = 256
DROP_DEV = 96
TOKENS = 1024
N_CTX = 4
N_TP = 8


def drop_counts(key):
    shards = TOKENS // TOK_DEV
    pair_total = shards // 2
    spread = jax.random.randint(jax.random.fold_in(key, 7), (pair_total,), 0, DROP_DEV + 1)
    widest = jax.random.randint(jax.random.fold_in(key, 8), (), 0, pair_total)
    spread = jnp.where(jnp.arange(pair_total) == widest, DROP_DEV, spread)
    heavy_first = jax.random.randint(jax.random.fold_in(key, 9), (pair_total,), 0, 2)
    first_drop = jnp.where(heavy_first == 1, DROP_DEV - spread, DROP_DEV + spread)
    second_drop = 2 * DROP_DEV - first_drop
    return jnp.stack([first_drop, second_drop], -1).reshape(shards).astype(jnp.int32)


def draw_kept_count(key, part):
    drop_list = drop_counts(key)
    return (TOK_DEV - drop_list).astype(jnp.int32)


def draw_keep_rows(key, part):
    drop_list = drop_counts(key)
    key = jax.random.fold_in(key, 5)
    shards = TOKENS // TOK_DEV
    rank_rows = jax.vmap(lambda sub_key: jax.random.permutation(sub_key, TOK_DEV))(jax.random.split(key, shards))
    dropped = (rank_rows < drop_list[:, None]).astype(jnp.int32)
    sort_key = dropped * TOK_DEV + jnp.arange(TOK_DEV, dtype=jnp.int32)[None, :]
    return jnp.argsort(sort_key, axis=1, stable=True).astype(jnp.int32).reshape(TOKENS)


def draw_positions(key, part):
    key = jax.random.fold_in(key, 3)
    step_size = jax.random.randint(key, (TOKENS,), 0, 2)
    step_size = step_size.at[0].set(0).at[TOKENS - 1].set(1)
    return (2 * jnp.arange(TOKENS, dtype=jnp.int32) + step_size).astype(jnp.int32)


def draw_residual(key, part):
    key = jax.random.fold_in(key, 11)
    column = 0.5 * jnp.power(3.0, jnp.arange(D, dtype=jnp.float32) / (D - 1))
    base_draw = jnp.clip(jax.random.normal(key, (TOKENS, D), jnp.float32), -4.0, 4.0)
    return (base_draw * column[None, :]).astype(jnp.bfloat16)


def draw_queries(key, part):
    key = jax.random.fold_in(key, 21)
    base_draw = jnp.clip(2.5 * jax.random.normal(key, (TOKENS, HQ, HD), jnp.float32), -15.0, 15.0)
    return base_draw.reshape(TOKENS, HQ * HD).astype(jnp.bfloat16)


def draw_keys_values(key, part):
    key = jax.random.fold_in(key, 31)
    base_draw = jnp.clip(jax.random.normal(key, (TOKENS, KVH, 2, HD), jnp.float32), -6.0, 6.0)
    return base_draw.reshape(TOKENS, KVH * 2 * HD).astype(jnp.bfloat16)


def with_spikes(result, own_key, source, target, shards_of, factor):
    owner, partner = [(jnp.arange(result.shape[dim]) // (result.shape[dim] // shards_of)).reshape([-1 if axis == dim else 1 for axis in range(result.ndim)]) for dim in (source, target)]
    chosen = jax.random.permutation(own_key, shards_of)[partner]
    strong = (owner == chosen) | (owner == (partner + shards_of // 2) % shards_of)
    return jnp.where(strong, factor * result, result)


def levels(key, extent, cuts, smallest, high):
    def one(axis_at, blocks):
        heights = jax.random.uniform(jax.random.fold_in(jax.random.fold_in(key, 6), axis_at), (blocks,), jnp.float32, smallest / len(cuts), high / len(cuts))
        return jnp.repeat(jnp.exp(heights), extent[axis_at] // blocks).reshape((-1,) + (1,) * (len(extent) - axis_at - 1))

    level = one(*cuts[0])
    for cut in cuts[1:]:
        level = level * one(*cut)
    return level


def gaussian(rng, shape, deviation, limit, pieces=(), held_as=jnp.bfloat16):
    drawn = jax.random.normal(rng, shape, jnp.float32) * deviation
    if len(pieces) > 0:
        drawn = levels(rng, shape, pieces, -0.22, 0.18) * drawn
    return jnp.clip(drawn, min=-limit, max=limit).astype(held_as)


def gaussian_with(key, dims, width, bound, cuts, heavy, held_as=jnp.bfloat16):
    array = width * jax.random.normal(key, dims, jnp.float32)
    if cuts:
        array = array * levels(key, dims, cuts, -0.22, 0.18)
    return jnp.clip(with_spikes(array, jax.random.fold_in(key, 3), *heavy), -bound, bound).astype(held_as)


def setup_inputs(seed: int = 0) -> dict:
    splits = jax.random.split(jax.random.key(seed), 10)
    residual = draw_residual(jax.random.fold_in(splits[9], 71), 0)
    queries = draw_queries(jax.random.fold_in(splits[9], 71), 0)
    keys_values = draw_keys_values(jax.random.fold_in(splits[9], 71), 0)
    out_weight = gaussian_with(splits[3], (HQ * HD, D), (HQ * HD) ** -0.5, 0.09375, ((0, 8), (1, 4)), (0, 1, 8, 2.0))
    norm_gain = jnp.clip(1.0 + 0.18 * jax.random.normal(splits[4], (D,), jnp.float32), 0.1, 1.9)
    cache_weight = gaussian(splits[5], (D, KVH * 2 * HD), D ** -0.5, 0.0625, ((1, 8),))
    positions = draw_positions(jax.random.fold_in(splits[9], 71), 0)
    keep_rows = draw_keep_rows(jax.random.fold_in(splits[9], 71), 0)
    kept_count = draw_kept_count(jax.random.fold_in(splits[9], 71), 0)
    return dict(residual=residual, queries=queries, keys_values=keys_values, out_weight=out_weight, norm_gain=norm_gain, cache_weight=cache_weight, positions=positions, keep_rows=keep_rows, kept_count=kept_count)


THETA = 1000000.0
EPS = 1e-06

def rotate_pairs(cache_rows, position_ids, first_col, head_dim):
    pair_count = cache_rows.shape[1] // 2
    columns = first_col + 2 * jnp.arange(pair_count, dtype=jnp.int32)
    within = columns % (2 * head_dim)
    is_key = within < head_dim
    exponent = jnp.where(is_key, within, 0).astype(jnp.float32) / head_dim
    frequency = jnp.power(jnp.float32(THETA), -exponent)
    angles = position_ids.astype(jnp.float32)[:, None] * frequency[None, :]
    paired = cache_rows.reshape(cache_rows.shape[0], pair_count, 2)
    first_half = paired[..., 0]
    second = paired[..., 1]
    cosine = jnp.cos(angles)
    sine_rows = jnp.sin(angles)
    turned_first = first_half * cosine - second * sine_rows
    turned_second = second * cosine + first_half * sine_rows
    turned = jnp.stack([jnp.where(is_key, turned_first, first_half), jnp.where(is_key, turned_second, second)], -1)
    return turned.reshape(cache_rows.shape)

def reference(residual, queries, keys_values, out_weight, norm_gain, cache_weight, positions, keep_rows, kept_count):
    group_size = HQ // KVH
    score_scale = 1.0 / math.sqrt(HD)
    query_heads = queries.reshape(TOKENS, HQ, HD).transpose(1, 0, 2)
    kv_pairs = keys_values.reshape(TOKENS, KVH, 2, HD)
    key_heads = kv_pairs[:, :, 0, :].transpose(1, 0, 2)
    value_heads = kv_pairs[:, :, 1, :].transpose(1, 0, 2)
    causal = jnp.arange(TOKENS, dtype=jnp.int32)[:, None] >= jnp.arange(TOKENS, dtype=jnp.int32)[None, :]

    def one_head(item_pair):
        query_rows, head_index = item_pair
        key_block = key_heads[head_index // group_size]
        value_block = value_heads[head_index // group_size]
        scores = jnp.dot(query_rows, key_block.T, preferred_element_type=jnp.float32) * score_scale
        scores = jnp.where(causal, scores, -jnp.inf)
        row_max = lax.optimization_barrier(jnp.max(scores, axis=-1, keepdims=True))
        probs = jnp.exp(scores - row_max)
        denominator = lax.optimization_barrier(jnp.sum(probs, axis=-1, keepdims=True))
        mixed_rows = jnp.dot(probs.astype(jnp.bfloat16), value_block, preferred_element_type=jnp.float32) / denominator
        return mixed_rows.astype(jnp.bfloat16)
    attended = lax.map(one_head, (query_heads, jnp.arange(HQ, dtype=jnp.int32)))
    attended = attended.transpose(1, 0, 2).reshape(TOKENS, HQ * HD)
    part_width = HQ * HD // N_TP
    attn_parts = attended.reshape(TOKENS, N_TP, part_width).transpose(1, 0, 2)
    weight_parts = out_weight.reshape(N_TP, part_width, D)

    def add_part(running, item_pair):
        attn_part, weight_part = item_pair
        term_part = jnp.dot(attn_part, weight_part, preferred_element_type=jnp.float32).astype(jnp.bfloat16)
        term_part = lax.optimization_barrier(term_part)
        return (running + term_part.astype(jnp.float32), None)
    summed, unused = lax.scan(add_part, jnp.zeros((TOKENS, D), jnp.float32), (attn_parts, weight_parts))
    hidden = (residual.astype(jnp.float32) + summed).astype(jnp.bfloat16)
    wide_hidden = hidden.astype(jnp.float32)
    inverse = lax.rsqrt(lax.optimization_barrier(jnp.mean(wide_hidden * wide_hidden, axis=-1, keepdims=True)) + EPS)
    normed = (wide_hidden * inverse * norm_gain[None, :]).astype(jnp.bfloat16)
    cache_rows = jnp.dot(normed, cache_weight, preferred_element_type=jnp.float32)
    cache_rot = rotate_pairs(cache_rows, positions, 0, HD).astype(jnp.bfloat16)
    keep_grid = keep_rows.reshape(N_CTX, TOK_DEV)
    valid_rows = (jnp.arange(TOK_DEV, dtype=jnp.int32)[None, :] < kept_count[:, None]).astype(jnp.int32)
    kept_flags = jnp.zeros((N_CTX, TOK_DEV), jnp.int32).at[jnp.arange(N_CTX, dtype=jnp.int32)[:, None], keep_grid].set(valid_rows)
    kept_rows = kept_flags.reshape(TOKENS)[:, None] > 0
    kept_hidden = jnp.where(kept_rows, hidden, jnp.zeros_like(hidden))
    kept_cache = jnp.where(kept_rows, cache_rot, jnp.zeros_like(cache_rot))
    return (kept_hidden, kept_cache)
```

```python
import math

import jax
import jax.numpy as jnp
from jax import lax
from jax.experimental import pallas as pl
from jax.experimental.pallas import tpu as pltpu
from jax.sharding import PartitionSpec as P

D = 8192
HQ = 64
KVH = 8
HD = 128


THETA = 1000000.0
EPS = 1e-06


def rotate_pairs(cache_rows, position_ids, first_col, head_dim):
    pair_count = cache_rows.shape[1] // 2
    columns = first_col + 2 * jnp.arange(pair_count, dtype=jnp.int32)
    within = columns % (2 * head_dim)
    is_key = within < head_dim
    exponent = jnp.where(is_key, within, 0).astype(jnp.float32) / head_dim
    frequency = jnp.power(jnp.float32(THETA), -exponent)
    angles = position_ids.astype(jnp.float32)[:, None] * frequency[None, :]
    paired = cache_rows.reshape(cache_rows.shape[0], pair_count, 2)
    first_half = paired[..., 0]
    second = paired[..., 1]
    cosine = jnp.cos(angles)
    sine_rows = jnp.sin(angles)
    turned_first = first_half * cosine - second * sine_rows
    turned_second = second * cosine + first_half * sine_rows
    turned = jnp.stack(
        [jnp.where(is_key, turned_first, first_half), jnp.where(is_key, turned_second, second)], -1
    )
    return turned.reshape(cache_rows.shape)


def shards(
    residual,
    queries,
    keys_values,
    out_weight,
    norm_gain,
    cache_weight,
    positions,
    keep_rows,
    kept_count,
):
    row_count = residual.shape[0]
    ctx_index = lax.axis_index("ctx")
    tp_index = lax.axis_index("tp")
    head_count = queries.shape[1] // HD
    kv_head = tp_index * head_count // (HQ // KVH)
    head_block = lax.dynamic_slice_in_dim(keys_values, kv_head * 2 * HD, 2 * HD, 1)
    key_rows = head_block[:, :HD]
    value_rows = head_block[:, HD:]
    query_rows = queries.reshape(row_count, head_count, HD)
    own_index = ctx_index * row_count + jnp.arange(row_count, dtype=jnp.int32)
    score_scale = 1.0 / math.sqrt(HD)
    running_max = jnp.full((row_count, head_count), -1e30, jnp.float32)
    key_block = lax.all_gather(key_rows, "ctx", axis=0, tiled=True)
    value_block = lax.all_gather(value_rows, "ctx", axis=0, tiled=True)
    block_rows = key_block.shape[0]
    scores = (
        jnp.einsum("rgd,kd->rgk", query_rows, key_block, preferred_element_type=jnp.float32)
        * score_scale
    )
    visible = jnp.arange(block_rows, dtype=jnp.int32)[None, :] <= own_index[:, None]
    visible = visible[:, None, :]
    scores = jnp.where(visible, scores, -1e30)
    new_max = jnp.maximum(running_max, jnp.max(scores, axis=-1))
    weights = jnp.where(visible, jnp.exp(scores - new_max[..., None]), 0.0)
    new_sum = jnp.sum(weights, axis=-1)
    update = jnp.einsum(
        "rgk,kd->rgd", weights.astype(jnp.bfloat16), value_block, preferred_element_type=jnp.float32
    )
    attended = (
        (update / new_sum[..., None]).reshape(row_count, head_count * HD).astype(jnp.bfloat16)
    )
    own_count = kept_count[0]
    valid_rows = jnp.arange(row_count, dtype=jnp.int32) < own_count
    partials = jnp.dot(
        attended,
        lax.all_gather(out_weight, "ctx", axis=1, tiled=True),
        preferred_element_type=jnp.float32,
    )
    group_sums = lax.psum_scatter(
        partials.astype(jnp.bfloat16), "tp", scatter_dimension=1, tiled=True
    ).astype(jnp.float32)
    hidden = (residual.astype(jnp.float32) + group_sums).astype(jnp.bfloat16)
    feat_width = hidden.shape[1]
    wide_hidden = hidden.astype(jnp.float32)
    square_total = lax.psum(jnp.sum(wide_hidden * wide_hidden, axis=-1), "tp")
    inverse = lax.rsqrt(square_total / D + EPS)
    gain_part = lax.dynamic_slice_in_dim(norm_gain, tp_index * feat_width, feat_width)
    normed = (wide_hidden * inverse[:, None] * gain_part[None, :]).astype(jnp.bfloat16)
    gathered = lax.all_gather(normed, "tp", axis=1, tiled=True)
    cache_rows = jnp.dot(gathered, cache_weight, preferred_element_type=jnp.float32)
    cache_rot = rotate_pairs(cache_rows, positions, tp_index * cache_rows.shape[1], HD).astype(
        jnp.bfloat16
    )
    kept_flags = jnp.zeros((row_count,), jnp.int32).at[keep_rows].set(valid_rows.astype(jnp.int32))
    kept_mask = kept_flags[:, None] > 0
    kept_hidden = jnp.where(kept_mask, hidden, jnp.zeros_like(hidden))
    kept_cache = jnp.where(kept_mask, cache_rot, jnp.zeros_like(cache_rot))
    return (kept_hidden, kept_cache)


KEPT = 160
Z = 4
MESH = pl.DeviceIdType.MESH
BF = jnp.bfloat16
F32 = jnp.float32


def fused_kernel(
    q_ref, r_ref, kv_hbm, w_hbm, cw_hbm, gain_ref, slot_row, slot_col,
    hid_out, cache_out,
    kvbuf, w_ref, cw_ref, qown, qrecv, rown, rrecv, resbuf, attb, ownp, ysend, yrecv,
    zsum, zrecv, hbuf, cmsg, crecv, cbuf, hpair,
    loc_sem, kv_s, kv_r, q_s, q_r, res_s, res_r, att_s, att_r, y_s, y_r, z_s, z_r,
    ag_s, ag_r, ay_s, ay_r, c_s, c_r, row_s, row_r, fin_s, fin_r,
):
    c = lax.axis_index("ctx")
    t = lax.axis_index("tp")
    p, k = c // 2, c % 2
    z, y = t // 2, t % 2
    rows = q_ref.shape[0]

    def ctx_peer(i):
        return ((p + i // 2) % 2) * 2 + (k + i % 2) % 2

    def z_peer(d):
        return (z + d) % Z

    sib = ctx_peer(1)
    ydev = (c, 2 * z + 1 - y)
    is_root = c == z
    pending = []

    def remote(src, dst, ss, rs, dev):
        return pltpu.make_async_remote_copy(
            src_ref=src, dst_ref=dst, send_sem=ss, recv_sem=rs, device_id=dev, device_id_type=MESH
        )

    def send(src, dst, ss, rs, dev):
        copy = remote(src, dst, ss, rs, dev)
        copy.start()
        pending.append(copy)
        return copy

    w_copy = pltpu.make_async_copy(w_hbm, w_ref, loc_sem.at[0])
    w_copy.start()
    feat = cw_ref.shape[0]
    cw_copy = pltpu.make_async_copy(
        cw_hbm.at[pl.ds(pl.multiple_of(c * feat, feat), feat)], cw_ref, loc_sem.at[1]
    )
    cw_copy.start()
    own_kv = kvbuf.at[pl.ds(pl.multiple_of(c * rows, rows), rows)]
    kv_copy = pltpu.make_async_copy(
        kv_hbm.at[:, pl.ds(pl.multiple_of(t * 2 * HD, 2 * HD), 2 * HD)], own_kv, loc_sem.at[2]
    )
    kv_copy.start()

    barrier = pltpu.get_barrier_semaphore()
    partners = [(ctx_peer(i), t) for i in (1, 2, 3)]
    partners += [(c, z_peer(d) * 2 + y) for d in (1, 2, 3)] + [ydev]
    for dev in partners:
        pl.semaphore_signal(barrier, inc=1, device_id=dev, device_id_type=MESH)
    pl.semaphore_wait(barrier, len(partners))

    slots = slot_row[...]
    slot_at = lax.broadcasted_iota(jnp.int32, (KEPT, rows), 0)
    pick_sib = jnp.where(slots == slot_at + (1 - k) * KEPT, 1.0, 0.0).astype(BF)
    pick_own = jnp.where(slots == slot_at + k * KEPT, 1.0, 0.0).astype(BF)
    row_id = lax.broadcasted_iota(jnp.int32, (rows, HD), 0).astype(F32)
    lane = lax.broadcasted_iota(jnp.int32, (rows, HD), 1)
    tags = jnp.where(lane == 0, row_id, jnp.where(lane == 1, 1.0, 0.0)).astype(BF)
    width = q_ref.shape[1]

    def pick(sel, what):
        return jnp.dot(sel, what, preferred_element_type=F32).astype(BF)

    kv_copy.wait()
    kv_copies = [
        send(own_kv, own_kv, kv_s.at[i - 1], kv_r.at[i - 1], (ctx_peer(i), t)) for i in (2, 3, 1)
    ]
    qown[0, :, :width] = pick(pick_sib, q_ref[...])
    qown[0, :, width:] = pick(pick_sib, tags)
    q_copy = send(qown.at[0], qrecv, q_s.at[0], q_r.at[0], (sib, t))
    rown[0] = pick(pick_sib, r_ref[...])
    r_copy = send(rown.at[0], rrecv, q_s.at[1], q_r.at[1], (sib, t))
    qown[1, :, :width] = pick(pick_own, q_ref[...])
    qown[1, :, width:] = pick(pick_own, tags)
    rown[1] = pick(pick_own, r_ref[...])

    q_copy.wait_recv()
    own_tag = qown[1, :, width:].astype(F32)
    sib_tag = qrecv[:, width:].astype(F32)
    first_own = (c * rows).astype(F32)
    first_sib = (sib * rows).astype(F32)
    limit = (
        own_tag[:, 0:1] + first_own * own_tag[:, 1:2] + sib_tag[:, 0:1] + first_sib * sib_tag[:, 1:2]
    )
    qown[1, :, :width] = qown[1, :, :width] + qrecv[:, :width]

    r_copy.wait_recv()
    rown[1] = rown[1] + rrecv[...]
    res_slot = ((p + z // 2) % 2) * 2 + (k + z) % 2
    res_copy = remote(
        rown.at[1], resbuf.at[res_slot], res_s, res_r.at[res_slot], (z, t)
    )

    @pl.when(is_root)
    def _():
        resbuf[0] = rown[1]

    @pl.when(jnp.logical_not(is_root))
    def _():
        res_copy.start()

    for copy in kv_copies:
        copy.wait_recv()
    total = kvbuf.shape[0]
    col_id = lax.broadcasted_iota(jnp.int32, (KEPT, total), 1).astype(F32)
    seen = col_id <= limit
    scale = 1.0 / math.sqrt(HD)
    keys = kvbuf[:, :HD]
    values = kvbuf[:, HD:]
    for h in range(width // HD):
        cols = slice(h * HD, (h + 1) * HD)
        s = lax.dot_general(
            qown[1, :, cols], keys, (((1,), (1,)), ((), ())), preferred_element_type=F32
        ) * scale
        s = jnp.where(seen, s, -1e30)
        top = jnp.max(s, axis=1, keepdims=True)
        e = jnp.where(seen, jnp.exp(s - top), 0.0)
        den = jnp.sum(e, axis=1, keepdims=True)
        mixed = jnp.dot(e.astype(BF), values, preferred_element_type=F32)
        attb[0, :, cols] = (mixed / den).astype(BF)

    att_cp = send(attb.at[0], attb.at[2], att_s.at[0], att_r.at[0], (ctx_peer(2), t))
    att_sib = send(attb.at[0], attb.at[1], att_s.at[1], att_r.at[1], (sib, t))
    half = Z * 256
    own_cols = pl.ds(pl.multiple_of(y * half, half), half)
    far_cols = pl.ds(pl.multiple_of((1 - y) * half, half), half)
    w_copy.wait()
    fwd = {}
    ys, zs, ags, ays, cs = {}, {}, {}, {}, {}

    def stage_a(i):
        if i == 1:
            att_sib.wait_recv()
        if i == 2:
            att_cp.wait_recv()
            fwd[0] = send(attb.at[2], attb.at[3], att_s.at[2], att_r.at[2], (sib, t))
        if i == 3:
            fwd[0].wait_recv()
        ysend[i] = jnp.dot(attb[i], w_ref[:, far_cols], preferred_element_type=F32).astype(BF)
        ys[i] = send(ysend.at[i], yrecv.at[i], y_s.at[i], y_r.at[i], ydev)
        ownp[i] = jnp.dot(attb[i], w_ref[:, own_cols], preferred_element_type=F32)

    def stage_b(i):
        ys[i].wait_recv()

        @pl.when(is_root)
        def _():
            if i > 0:
                remote(
                    rown.at[1], resbuf.at[i], res_s, res_r.at[i], (ctx_peer(i), t)
                ).wait_recv()
            ownp[i] = ownp[i] + resbuf[i].astype(F32)

        for j in range(Z):
            cols = slice(j * 256, (j + 1) * 256)
            zsum[i, j] = (ownp[i, :, cols] + yrecv[i, :, cols].astype(F32)).astype(BF)
        for d in (2, 1, 3):
            zs[i, d] = send(
                zsum.at[i, z_peer(d)], zrecv.at[i, d - 1], z_s.at[i, d - 1], z_r.at[i, d - 1],
                (c, z_peer(d) * 2 + y),
            )

    def stage_c(i):
        for d in (1, 2, 3):
            zs[i, d].wait_recv()
        hid = zsum[i, z].astype(F32)
        for d in range(Z - 1):
            hid = hid + zrecv[i, d].astype(F32)
        hbuf[i, y, z] = hid.astype(BF)
        for d in (2, 1, 3):
            ags[i, d] = send(
                hbuf.at[i, y, z], hbuf.at[i, y, z], ag_s.at[i, d - 1], ag_r.at[i, d - 1],
                (c, z_peer(d) * 2 + y),
            )

    def row_copy(i):
        return remote(
            hbuf.at[i, y], hpair.at[(k + i % 2) % 2], row_s.at[i], row_r, (ctx_peer(i), t)
        )

    def stage_d(i):
        for d in (1, 2, 3):
            ags[i, d].wait_recv()
        ays[i] = send(hbuf.at[i, y], hbuf.at[i, y], ay_s.at[i], ay_r.at[i], ydev)

        @pl.when(is_root)
        def _():
            if i == 0:
                hpair[k] = hbuf[i, y]
            else:
                row_copy(i).start()

    gains = gain_ref[c]

    def stage_e(i):
        ays[i].wait_recv()
        acc = jnp.zeros((KEPT, 256), F32)
        squares = jnp.zeros((KEPT, 1), F32)
        for q in range(2 * Z):
            wide = hbuf[i, q // Z, q % Z].astype(F32)
            squares = squares + jnp.sum(wide * wide, axis=1, keepdims=True)
            acc = acc + jnp.dot(
                (wide * gains[q : q + 1, :]).astype(BF),
                cw_ref[q * 256 : (q + 1) * 256, :],
                preferred_element_type=F32,
            )
        if i == 0:
            return acc, squares
        coarse = squares.astype(BF).astype(F32)
        at = lax.broadcasted_iota(jnp.int32, (KEPT, HD), 1)
        cmsg[i - 1, :, :256] = acc.astype(BF)
        cmsg[i - 1, :, 256:] = jnp.where(
            at == 0, coarse, jnp.where(at == 1, squares - coarse, 0.0)
        ).astype(BF)
        cs[i] = send(
            cmsg.at[i - 1], crecv.at[i - 1], c_s.at[i - 1], c_r.at[i - 1], (ctx_peer(i), t)
        )
        return None

    stage_a(0)
    stage_a(1)
    stage_b(0)
    stage_a(2)
    stage_b(1)
    stage_c(0)
    stage_a(3)
    stage_b(2)
    stage_c(1)
    stage_d(0)
    stage_b(3)
    stage_c(2)
    stage_d(1)
    cw_copy.wait()
    acc, squares = stage_e(0)
    stage_c(3)
    stage_d(2)
    stage_e(1)
    stage_d(3)
    stage_e(2)

    @pl.when(jnp.logical_not(is_root))
    def _():
        row_copy(1).wait_recv()

    pair_copy = send(hpair.at[k], hpair.at[k], fin_s.at[0], fin_r.at[0], (sib, t))
    stage_e(3)
    slots_c = slot_col[...]
    place_at = lax.broadcasted_iota(jnp.int32, (rows, KEPT), 1)
    place = [jnp.where(slots_c == place_at + kk * KEPT, 1.0, 0.0).astype(BF) for kk in range(2)]
    pair_copy.wait_recv()
    for j in range(Z):
        hid_out[:, j * 256 : (j + 1) * 256] = (
            jnp.dot(place[0], hpair[0, j], preferred_element_type=F32)
            + jnp.dot(place[1], hpair[1, j], preferred_element_type=F32)
        ).astype(BF)
    for i in (1, 2, 3):
        cs[i].wait_recv()
        got = crecv[i - 1, :, 256:].astype(F32)
        acc = acc + crecv[i - 1, :, :256].astype(F32)
        squares = squares + got[:, 0:1] + got[:, 1:2]
    cbuf[k] = (acc * lax.rsqrt(squares / D + EPS)).astype(BF)
    last = send(cbuf.at[k], cbuf.at[k], fin_s.at[1], fin_r.at[1], (sib, t))
    last.wait_recv()
    cache_out[...] = (
        jnp.dot(place[0], cbuf[0], preferred_element_type=F32)
        + jnp.dot(place[1], cbuf[1], preferred_element_type=F32)
    ).astype(BF)

    for copy in pending:
        copy.wait_send()

    @pl.when(jnp.logical_not(is_root))
    def _():
        res_copy.wait_send()

    @pl.when(is_root)
    def _():
        for i in (1, 2, 3):
            row_copy(i).wait_send()


def rotate_head(raw, position_ids):
    column = jnp.arange(raw.shape[1], dtype=jnp.int32)
    within = column - column % 2
    is_key = column < HD
    exponent = jnp.where(is_key, within, 0).astype(F32) / HD
    frequency = jnp.power(jnp.float32(THETA), -exponent)
    angles = position_ids.astype(F32)[:, None] * frequency[None, :]
    cosine = jnp.where(is_key, jnp.cos(angles), 1.0)
    sine = jnp.where(is_key, jnp.sin(angles), 0.0)
    partner = jnp.where(column % 2 == 0, -jnp.roll(raw, -1, axis=1), jnp.roll(raw, 1, axis=1))
    return raw * cosine + partner * sine


def fused_shards(
    residual, queries, keys_values, out_weight, norm_gain, cache_weight, positions, keep_rows, kept_count
):
    rows, width = queries.shape
    ctx_index = lax.axis_index("ctx")
    own_count = kept_count[0]
    base = jnp.where(ctx_index % 2 == 0, 0, 2 * KEPT - own_count)
    order = jnp.arange(rows, dtype=jnp.int32)
    at = jnp.where(order < own_count, base + order + 1, 0)
    slot = jnp.sum(jnp.where(keep_rows[None, :] == order[:, None], at[None, :], 0), axis=1) - 1
    feat = out_weight.shape[1]
    n_ctx = D // feat
    dma = pltpu.SemaphoreType.DMA
    vmem = pl.BlockSpec(memory_space=pltpu.VMEM)
    hbm = pl.BlockSpec(memory_space=pl.ANY)
    kept_hidden, raw = pl.pallas_call(
        fused_kernel,
        out_shape=(
            jax.ShapeDtypeStruct((rows, width), BF),
            jax.ShapeDtypeStruct((rows, 2 * HD), BF),
        ),
        in_specs=[vmem, vmem, hbm, hbm, hbm, vmem, vmem, vmem],
        out_specs=(vmem, vmem),
        scratch_shapes=[
            pltpu.VMEM((n_ctx * rows, 2 * HD), BF),
            pltpu.VMEM(out_weight.shape, BF),
            pltpu.VMEM((feat, 2 * HD), BF),
            pltpu.VMEM((2, KEPT, width + HD), BF),
            pltpu.VMEM((KEPT, width + HD), BF),
            pltpu.VMEM((2, KEPT, width), BF),
            pltpu.VMEM((KEPT, width), BF),
            pltpu.VMEM((4, KEPT, width), BF),
            pltpu.VMEM((4, KEPT, width), BF),
            pltpu.VMEM((4, KEPT, width), F32),
            pltpu.VMEM((4, KEPT, width), BF),
            pltpu.VMEM((4, KEPT, width), BF),
            pltpu.VMEM((4, Z, KEPT, 256), BF),
            pltpu.VMEM((4, Z - 1, KEPT, 256), BF),
            pltpu.VMEM((4, 2, Z, KEPT, 256), BF),
            pltpu.VMEM((3, KEPT, 256 + HD), BF),
            pltpu.VMEM((3, KEPT, 256 + HD), BF),
            pltpu.VMEM((2, KEPT, 256), BF),
            pltpu.VMEM((2, Z, KEPT, 256), BF),
            dma((3,)), dma((3,)), dma((3,)), dma((2,)), dma((2,)), dma, dma((4,)),
            dma((3,)), dma((3,)), dma((4,)), dma((4,)), dma((4, 3)), dma((4, 3)),
            dma((4, 3)), dma((4, 3)), dma((4,)), dma((4,)), dma((3,)), dma((3,)),
            dma((4,)), dma, dma((2,)), dma((2,)),
        ],
        compiler_params=pltpu.CompilerParams(
            collective_id=0, has_side_effects=True, vmem_limit_bytes=48 * 1024 * 1024
        ),
        cost_estimate=pl.CostEstimate(flops=6_000_000_000, bytes_accessed=8_000_000, transcendentals=1_400_000),
    )(
        queries, residual, keys_values, out_weight, cache_weight,
        norm_gain.reshape(n_ctx, feat // 256, 256), slot[None, :], slot[:, None],
    )
    kept_cache = rotate_head(raw.astype(F32), positions).astype(BF)
    return (kept_hidden, kept_cache)


def solution(mesh):
    in_specs = (
        P("ctx", "tp"),
        P("ctx", "tp"),
        P("ctx", None),
        P("tp", "ctx"),
        P(),
        P(None, "tp"),
        P("ctx"),
        P("ctx"),
        P("ctx"),
    )
    out_specs = (P("ctx", "tp"), P("ctx", "tp"))
    fits = mesh.shape["ctx"] == 4 and mesh.shape["tp"] == 8
    body = fused_shards if fits else shards
    return jax.shard_map(body, mesh=mesh, in_specs=in_specs, out_specs=out_specs, check_vma=False)
```

```python
import math

import jax
import jax.numpy as jnp
from jax import lax
from jax.experimental import pallas as pl
from jax.experimental.pallas import tpu as pltpu
from jax.sharding import PartitionSpec as P

D = 8192
HQ = 64
KVH = 8
HD = 128


THETA = 1000000.0
EPS = 1e-06


def rotate_pairs(cache_rows, position_ids, first_col, head_dim):
    pair_count = cache_rows.shape[1] // 2
    columns = first_col + 2 * jnp.arange(pair_count, dtype=jnp.int32)
    within = columns % (2 * head_dim)
    is_key = within < head_dim
    exponent = jnp.where(is_key, within, 0).astype(jnp.float32) / head_dim
    frequency = jnp.power(jnp.float32(THETA), -exponent)
    angles = position_ids.astype(jnp.float32)[:, None] * frequency[None, :]
    paired = cache_rows.reshape(cache_rows.shape[0], pair_count, 2)
    first_half = paired[..., 0]
    second = paired[..., 1]
    cosine = jnp.cos(angles)
    sine_rows = jnp.sin(angles)
    turned_first = first_half * cosine - second * sine_rows
    turned_second = second * cosine + first_half * sine_rows
    turned = jnp.stack(
        [jnp.where(is_key, turned_first, first_half), jnp.where(is_key, turned_second, second)], -1
    )
    return turned.reshape(cache_rows.shape)


def shards(
    residual,
    queries,
    keys_values,
    out_weight,
    norm_gain,
    cache_weight,
    positions,
    keep_rows,
    kept_count,
):
    row_count = residual.shape[0]
    ctx_index = lax.axis_index("ctx")
    tp_index = lax.axis_index("tp")
    head_count = queries.shape[1] // HD
    kv_head = tp_index * head_count // (HQ // KVH)
    head_block = lax.dynamic_slice_in_dim(keys_values, kv_head * 2 * HD, 2 * HD, 1)
    key_rows = head_block[:, :HD]
    value_rows = head_block[:, HD:]
    query_rows = queries.reshape(row_count, head_count, HD)
    own_index = ctx_index * row_count + jnp.arange(row_count, dtype=jnp.int32)
    score_scale = 1.0 / math.sqrt(HD)
    running_max = jnp.full((row_count, head_count), -1e30, jnp.float32)
    key_block = lax.all_gather(key_rows, "ctx", axis=0, tiled=True)
    value_block = lax.all_gather(value_rows, "ctx", axis=0, tiled=True)
    block_rows = key_block.shape[0]
    scores = (
        jnp.einsum("rgd,kd->rgk", query_rows, key_block, preferred_element_type=jnp.float32)
        * score_scale
    )
    visible = jnp.arange(block_rows, dtype=jnp.int32)[None, :] <= own_index[:, None]
    visible = visible[:, None, :]
    scores = jnp.where(visible, scores, -1e30)
    new_max = jnp.maximum(running_max, jnp.max(scores, axis=-1))
    weights = jnp.where(visible, jnp.exp(scores - new_max[..., None]), 0.0)
    new_sum = jnp.sum(weights, axis=-1)
    update = jnp.einsum(
        "rgk,kd->rgd", weights.astype(jnp.bfloat16), value_block, preferred_element_type=jnp.float32
    )
    attended = (
        (update / new_sum[..., None]).reshape(row_count, head_count * HD).astype(jnp.bfloat16)
    )
    own_count = kept_count[0]
    valid_rows = jnp.arange(row_count, dtype=jnp.int32) < own_count
    partials = jnp.dot(
        attended,
        lax.all_gather(out_weight, "ctx", axis=1, tiled=True),
        preferred_element_type=jnp.float32,
    )
    group_sums = lax.psum_scatter(
        partials.astype(jnp.bfloat16), "tp", scatter_dimension=1, tiled=True
    ).astype(jnp.float32)
    hidden = (residual.astype(jnp.float32) + group_sums).astype(jnp.bfloat16)
    feat_width = hidden.shape[1]
    wide_hidden = hidden.astype(jnp.float32)
    square_total = lax.psum(jnp.sum(wide_hidden * wide_hidden, axis=-1), "tp")
    inverse = lax.rsqrt(square_total / D + EPS)
    gain_part = lax.dynamic_slice_in_dim(norm_gain, tp_index * feat_width, feat_width)
    normed = (wide_hidden * inverse[:, None] * gain_part[None, :]).astype(jnp.bfloat16)
    gathered = lax.all_gather(normed, "tp", axis=1, tiled=True)
    cache_rows = jnp.dot(gathered, cache_weight, preferred_element_type=jnp.float32)
    cache_rot = rotate_pairs(cache_rows, positions, tp_index * cache_rows.shape[1], HD).astype(
        jnp.bfloat16
    )
    kept_flags = jnp.zeros((row_count,), jnp.int32).at[keep_rows].set(valid_rows.astype(jnp.int32))
    kept_mask = kept_flags[:, None] > 0
    kept_hidden = jnp.where(kept_mask, hidden, jnp.zeros_like(hidden))
    kept_cache = jnp.where(kept_mask, cache_rot, jnp.zeros_like(cache_rot))
    return (kept_hidden, kept_cache)


KEPT = 160
Z = 4
MESH = pl.DeviceIdType.MESH
BF = jnp.bfloat16
F32 = jnp.float32


def fused_kernel(
    q_hbm, r_hbm, kv_hbm, w_hbm, cw_hbm, gain_ref, keep_ref, count_ref,
    hid_out, cache_out,
    q_ref, r_ref, kvbuf, w_ref, cw_ref, qown, qrecv, rown, rrecv, resbuf, attb, ownp, ysend, yrecv,
    zsum, zrecv, hbuf, ymsg, ymsg_in, cmsg, crecv, cbuf, hpair,
    loc_sem, kv_s, kv_r, q_s, q_r, res_s, res_r, att_s, att_r, y_s, y_r, z_s, z_r,
    ag_s, ag_r, fw_s, ay_s, ay_r, cw_s, cw_r, c_s, c_r, row_s, row_r, fin_s, fin_r,
):
    c = lax.axis_index("ctx")
    t = lax.axis_index("tp")
    p, k = c // 2, c % 2
    z, y = t // 2, t % 2
    rows = q_ref.shape[0]
    near = z + 1 - 2 * (z % 2)
    cross = 2 - z // 2
    is_inner = (z + 1) // 2 == 1

    def ctx_peer(i):
        return ((p + i // 2) % 2) * 2 + (k + i % 2) % 2

    def z_peer(d):
        return (z + d) % Z

    sib = ctx_peer(1)
    ydev = (c, 2 * z + 1 - y)
    is_root = c == z
    pending = []

    def remote(src, dst, ss, rs, dev):
        return pltpu.make_async_remote_copy(
            src_ref=src, dst_ref=dst, send_sem=ss, recv_sem=rs, device_id=dev, device_id_type=MESH
        )

    def send(src, dst, ss, rs, dev):
        copy = remote(src, dst, ss, rs, dev)
        copy.start()
        pending.append(copy)
        return copy

    feat = cw_ref.shape[1]
    own_kv = kvbuf.at[pl.ds(pl.multiple_of(c * rows, rows), rows)]
    kv_copy = pltpu.make_async_copy(
        kv_hbm.at[:, pl.ds(pl.multiple_of(t * 2 * HD, 2 * HD), 2 * HD)], own_kv, loc_sem.at[2]
    )
    kv_copy.start()
    q_load = pltpu.make_async_copy(q_hbm, q_ref, loc_sem.at[3])
    q_load.start()
    r_load = pltpu.make_async_copy(r_hbm, r_ref, loc_sem.at[4])
    r_load.start()
    w_copy = pltpu.make_async_copy(w_hbm, w_ref, loc_sem.at[0])
    w_copy.start()
    first_feat = pl.multiple_of((2 * c + y) * feat, feat)
    cw_copy = pltpu.make_async_copy(cw_hbm.at[pl.ds(first_feat, feat)], cw_ref.at[0], loc_sem.at[1])
    cw_copy.start()

    barrier = pltpu.get_barrier_semaphore()
    partners = [(ctx_peer(i), t) for i in (1, 2, 3)]
    partners += [(c, z_peer(d) * 2 + y) for d in (1, 2, 3)] + [ydev]
    for dev in partners:
        pl.semaphore_signal(barrier, inc=1, device_id=dev, device_id_type=MESH)
    pl.semaphore_wait(barrier, len(partners))

    count = count_ref[...]
    base = jnp.where(k == 0, 0, 2 * KEPT - count)
    chosen = keep_ref[...] == lax.broadcasted_iota(jnp.int32, (rows, rows), 0)
    rank = lax.broadcasted_iota(jnp.int32, (rows, KEPT), 0)
    slot_at = lax.broadcasted_iota(jnp.int32, (rows, KEPT), 1)
    chosen = jnp.where(chosen, 1.0, 0.0).astype(BF)

    def place_of(kk):
        hit = (rank + base == slot_at + kk * KEPT) & (rank < count)
        return jnp.dot(
            chosen, jnp.where(hit, 1.0, 0.0).astype(BF), preferred_element_type=F32
        ).astype(BF)

    place_sib = place_of(1 - k)
    place_own = place_of(k)
    row_id = lax.broadcasted_iota(jnp.int32, (rows, HD), 0).astype(F32)
    lane = lax.broadcasted_iota(jnp.int32, (rows, HD), 1)
    tags = jnp.where(lane == 0, row_id, jnp.where(lane == 1, 1.0, 0.0)).astype(BF)
    width = q_ref.shape[1]

    def pick(sel, what):
        return lax.dot_general(
            sel, what, (((0,), (0,)), ((), ())), preferred_element_type=F32
        ).astype(BF)

    kv_copy.wait()
    kv_far = send(own_kv, own_kv, kv_s.at[0], kv_r.at[0], (ctx_peer(2), t))
    kv_sib = send(own_kv, own_kv, kv_s.at[1], kv_r.at[1], (sib, t))
    cw_send = send(
        cw_hbm.at[pl.ds(pl.multiple_of((2 * c + 1 - y) * feat, feat), feat)],
        cw_ref.at[1], cw_s, cw_r, ydev,
    )
    q_load.wait()
    qown[0, :, :width] = pick(place_sib, q_ref[...])
    qown[0, :, width:] = pick(place_sib, tags)
    q_copy = send(qown.at[0], qrecv, q_s.at[0], q_r.at[0], (sib, t))
    r_load.wait()
    rown[0] = pick(place_sib, r_ref[...])
    r_copy = send(rown.at[0], rrecv, q_s.at[1], q_r.at[1], (sib, t))
    qown[1, :, :width] = pick(place_own, q_ref[...])
    qown[1, :, width:] = pick(place_own, tags)
    rown[1] = pick(place_own, r_ref[...])

    kv_far.wait_recv()
    far_kv = kvbuf.at[pl.ds(pl.multiple_of(ctx_peer(2) * rows, rows), rows)]
    kv_diag = send(far_kv, far_kv, kv_s.at[2], kv_r.at[2], (sib, t))
    q_copy.wait_recv()
    own_tag = qown[1, :, width:].astype(F32)
    sib_tag = qrecv[:, width:].astype(F32)
    first_own = (c * rows).astype(F32)
    first_sib = (sib * rows).astype(F32)
    limit = (
        own_tag[:, 0:1] + first_own * own_tag[:, 1:2] + sib_tag[:, 0:1] + first_sib * sib_tag[:, 1:2]
    )
    qown[1, :, :width] = qown[1, :, :width] + qrecv[:, :width]

    r_copy.wait_recv()
    rown[1] = rown[1] + rrecv[...]
    res_slot = ((p + z // 2) % 2) * 2 + (k + z) % 2
    res_copy = remote(
        rown.at[1], resbuf.at[res_slot], res_s, res_r.at[res_slot], (z, t)
    )

    @pl.when(is_root)
    def _():
        resbuf[0] = rown[1]

    @pl.when(jnp.logical_not(is_root))
    def _():
        res_copy.start()

    kv_sib.wait_recv()
    kv_diag.wait_recv()
    total = kvbuf.shape[0]
    col_id = lax.broadcasted_iota(jnp.int32, (KEPT, total), 1).astype(F32)
    seen = col_id <= limit
    scale = 1.0 / math.sqrt(HD)
    keys = kvbuf[:, :HD]
    values = kvbuf[:, HD:]
    for h in range(width // HD):
        cols = slice(h * HD, (h + 1) * HD)
        s = lax.dot_general(
            qown[1, :, cols], keys, (((1,), (1,)), ((), ())), preferred_element_type=F32
        ) * scale
        s = jnp.where(seen, s, -1e30)
        top = jnp.max(s, axis=1, keepdims=True)
        e = jnp.exp(s - top)
        den = jnp.sum(e, axis=1, keepdims=True)
        mixed = jnp.dot(e.astype(BF), values, preferred_element_type=F32)
        attb[0, :, cols] = (mixed / den).astype(BF)

    att_cp = send(attb.at[0], attb.at[2], att_s.at[0], att_r.at[0], (ctx_peer(2), t))
    att_sib = send(attb.at[0], attb.at[1], att_s.at[1], att_r.at[1], (sib, t))
    half = Z * 256
    own_cols = pl.ds(pl.multiple_of(y * half, half), half)
    far_cols = pl.ds(pl.multiple_of((1 - y) * half, half), half)
    w_copy.wait()
    fwd = {}
    ys, zs, ags, ays, cs = {}, {}, {}, {}, {}

    def stage_a(i):
        if i == 1:
            att_sib.wait_recv()
        if i == 2:
            att_cp.wait_recv()
            fwd[0] = send(attb.at[2], attb.at[3], att_s.at[2], att_r.at[2], (sib, t))
        if i == 3:
            fwd[0].wait_recv()
        ysend[i] = jnp.dot(attb[i], w_ref[:, far_cols], preferred_element_type=F32).astype(BF)
        ys[i] = send(ysend.at[i], yrecv.at[i], y_s.at[i], y_r.at[i], ydev)
        ownp[i] = jnp.dot(attb[i], w_ref[:, own_cols], preferred_element_type=F32)

    def stage_b(i):
        ys[i].wait_recv()

        @pl.when(is_root)
        def _():
            if i > 0:
                remote(
                    rown.at[1], resbuf.at[i], res_s, res_r.at[i], (ctx_peer(i), t)
                ).wait_recv()
            ownp[i] = ownp[i] + resbuf[i].astype(F32)

        for j in range(Z):
            cols = slice(j * 256, (j + 1) * 256)
            zsum[i, j] = (ownp[i, :, cols] + yrecv[i, :, cols].astype(F32)).astype(BF)
        for d in (2, 1, 3):
            zs[i, d] = send(
                zsum.at[i, z_peer(d)], zrecv.at[i, d - 1], z_s.at[i, d - 1], z_r.at[i, d - 1],
                (c, z_peer(d) * 2 + y),
            )

    def stage_c(i):
        for d in (1, 2, 3):
            zs[i, d].wait_recv()
        hid = zsum[i, z].astype(F32)
        for d in range(Z - 1):
            hid = hid + zrecv[i, d].astype(F32)
        hbuf[i, z] = hid.astype(BF)
        piece = hbuf.at[i, z]
        ags[i, 0] = send(piece, piece, ag_s.at[i, 0], ag_r.at[i, z], (c, cross * 2 + y))
        ags[i, 1] = send(piece, piece, ag_s.at[i, 1], ag_r.at[i, z], (c, near * 2 + y))

    def piece_copy(i, zz):
        piece = hbuf.at[i, zz]
        return remote(piece, piece, fw_s.at[i, zz % 2], ag_r.at[i, zz], (c, near * 2 + y))

    other = 2 * (1 - z // 2)

    def stage_f(i):
        @pl.when(is_inner)
        def _():
            for j in range(2):
                piece_copy(i, other + j).wait_recv()
                piece_copy(i, other + j).start()

    def row_copy(i):
        return remote(
            hbuf.at[i], hpair.at[(k + i % 2) % 2], row_s.at[i], row_r, (ctx_peer(i), t)
        )

    own_part = {}

    def packed(acc, squares):
        coarse = squares.astype(BF).astype(F32)
        at = lax.broadcasted_iota(jnp.int32, (KEPT, HD), 1)
        tail = jnp.where(at == 0, coarse, jnp.where(at == 1, squares - coarse, 0.0))
        return acc.astype(BF), tail.astype(BF)

    def unpacked(ref, i):
        tail = ref[i, :, 256:].astype(F32)
        return ref[i, :, :256].astype(F32), tail[:, 0:1] + tail[:, 1:2]

    def stage_d(i):
        piece_copy(i, near).wait_recv()

        @pl.when(jnp.logical_not(is_inner))
        def _():
            for j in range(2):
                piece_copy(i, other + j).wait_recv()

        @pl.when(is_root)
        def _():
            if i == 0:
                hpair[k] = hbuf[i]
            else:
                row_copy(i).start()

        if i == 0:
            cw_copy.wait()
            cw_send.wait_recv()
        far = jnp.zeros((KEPT, 256), F32)
        acc = jnp.zeros((KEPT, 256), F32)
        squares = jnp.zeros((KEPT, 1), F32)
        for q in range(Z):
            wide = hbuf[i, q].astype(F32)
            squares = squares + jnp.sum(wide * wide, axis=1, keepdims=True)
            gain = gain_ref[:, pl.ds(pl.multiple_of(first_feat + q * 256, 256), 256)]
            scaled = (wide * gain).astype(BF)
            cut = slice(q * 256, (q + 1) * 256)
            far = far + jnp.dot(scaled, cw_ref[1, cut], preferred_element_type=F32)
            acc = acc + jnp.dot(scaled, cw_ref[0, cut], preferred_element_type=F32)
        ymsg[i, :, :256], ymsg[i, :, 256:] = packed(far, squares)
        ays[i] = send(ymsg.at[i], ymsg_in.at[i], ay_s.at[i], ay_r.at[i], ydev)
        own_part[i] = acc, squares

    def stage_e(i):
        ays[i].wait_recv()
        acc, squares = own_part[i]
        more, more_squares = unpacked(ymsg_in, i)
        acc = acc + more
        squares = squares + more_squares
        if i == 0:
            return acc, squares
        cmsg[i - 1, :, :256], cmsg[i - 1, :, 256:] = packed(acc, squares)
        cs[i] = send(
            cmsg.at[i - 1], crecv.at[i - 1], c_s.at[i - 1], c_r.at[i - 1], (ctx_peer(i), t)
        )
        return None

    stage_a(0)
    stage_a(1)
    stage_b(0)
    stage_a(2)
    stage_b(1)
    stage_c(0)
    stage_a(3)
    stage_b(2)
    stage_c(1)
    stage_f(0)
    stage_b(3)
    stage_c(2)
    stage_f(1)
    stage_d(0)
    stage_c(3)
    stage_f(2)
    stage_d(1)
    stage_f(3)
    stage_d(2)
    stage_e(1)
    stage_d(3)
    stage_e(2)

    @pl.when(jnp.logical_not(is_root))
    def _():
        row_copy(1).wait_recv()

    pair_copy = send(hpair.at[k], hpair.at[k], fin_s.at[0], fin_r.at[0], (sib, t))
    stage_e(3)
    acc, squares = stage_e(0)
    place = [place_of(kk) for kk in range(2)]
    pair_copy.wait_recv()
    for j in range(Z):
        hid_out[:, j * 256 : (j + 1) * 256] = (
            jnp.dot(place[0], hpair[0, j], preferred_element_type=F32)
            + jnp.dot(place[1], hpair[1, j], preferred_element_type=F32)
        ).astype(BF)
    for i in (1, 2, 3):
        cs[i].wait_recv()
        more, more_squares = unpacked(crecv, i - 1)
        acc = acc + more
        squares = squares + more_squares
    cbuf[k] = (acc * lax.rsqrt(squares / D + EPS)).astype(BF)
    last = send(cbuf.at[k], cbuf.at[k], fin_s.at[1], fin_r.at[1], (sib, t))
    last.wait_recv()
    cache_out[...] = (
        jnp.dot(place[0], cbuf[0], preferred_element_type=F32)
        + jnp.dot(place[1], cbuf[1], preferred_element_type=F32)
    ).astype(BF)

    for copy in pending:
        copy.wait_send()

    @pl.when(jnp.logical_not(is_root))
    def _():
        res_copy.wait_send()

    @pl.when(is_root)
    def _():
        for i in (1, 2, 3):
            row_copy(i).wait_send()

    @pl.when(is_inner)
    def _():
        for i in range(4):
            for j in range(2):
                piece_copy(i, other + j).wait_send()


def rotate_head(raw, position_ids):
    column = jnp.arange(raw.shape[1], dtype=jnp.int32)
    within = column - column % 2
    is_key = column < HD
    exponent = jnp.where(is_key, within, 0).astype(F32) / HD
    frequency = jnp.power(jnp.float32(THETA), -exponent)
    angles = position_ids.astype(F32)[:, None] * frequency[None, :]
    cosine = jnp.where(is_key, jnp.cos(angles), 1.0)
    sine = jnp.where(is_key, jnp.sin(angles), 0.0)
    partner = jnp.where(column % 2 == 0, -jnp.roll(raw, -1, axis=1), jnp.roll(raw, 1, axis=1))
    return raw * cosine + partner * sine


def fused_shards(
    residual, queries, keys_values, out_weight, norm_gain, cache_weight, positions, keep_rows, kept_count
):
    rows, width = queries.shape
    feat = out_weight.shape[1]
    n_ctx = D // feat
    dma = pltpu.SemaphoreType.DMA
    vmem = pl.BlockSpec(memory_space=pltpu.VMEM)
    hbm = pl.BlockSpec(memory_space=pl.ANY)
    kept_hidden, raw = pl.pallas_call(
        fused_kernel,
        out_shape=(
            jax.ShapeDtypeStruct((rows, width), BF),
            jax.ShapeDtypeStruct((rows, 2 * HD), BF),
        ),
        in_specs=[hbm, hbm, hbm, hbm, hbm, vmem, vmem, vmem],
        out_specs=(vmem, vmem),
        scratch_shapes=[
            pltpu.VMEM((rows, width), BF),
            pltpu.VMEM((rows, width), BF),
            pltpu.VMEM((n_ctx * rows, 2 * HD), BF),
            pltpu.VMEM(out_weight.shape, BF),
            pltpu.VMEM((2, feat // 2, 2 * HD), BF),
            pltpu.VMEM((2, KEPT, width + HD), BF),
            pltpu.VMEM((KEPT, width + HD), BF),
            pltpu.VMEM((2, KEPT, width), BF),
            pltpu.VMEM((KEPT, width), BF),
            pltpu.VMEM((4, KEPT, width), BF),
            pltpu.VMEM((4, KEPT, width), BF),
            pltpu.VMEM((4, KEPT, width), F32),
            pltpu.VMEM((4, KEPT, width), BF),
            pltpu.VMEM((4, KEPT, width), BF),
            pltpu.VMEM((4, Z, KEPT, 256), BF),
            pltpu.VMEM((4, Z - 1, KEPT, 256), BF),
            pltpu.VMEM((4, Z, KEPT, 256), BF),
            pltpu.VMEM((4, KEPT, 256 + HD), BF),
            pltpu.VMEM((4, KEPT, 256 + HD), BF),
            pltpu.VMEM((3, KEPT, 256 + HD), BF),
            pltpu.VMEM((3, KEPT, 256 + HD), BF),
            pltpu.VMEM((2, KEPT, 256), BF),
            pltpu.VMEM((2, Z, KEPT, 256), BF),
            dma((5,)), dma((3,)), dma((3,)), dma((2,)), dma((2,)), dma, dma((4,)),
            dma((3,)), dma((3,)), dma((4,)), dma((4,)), dma((4, 3)), dma((4, 3)),
            dma((4, 2)), dma((4, 4)), dma((4, 2)), dma((4,)), dma((4,)), dma, dma, dma((3,)), dma((3,)),
            dma((4,)), dma, dma((2,)), dma((2,)),
        ],
        compiler_params=pltpu.CompilerParams(
            collective_id=0, has_side_effects=True, vmem_limit_bytes=48 * 1024 * 1024
        ),
        cost_estimate=pl.CostEstimate(flops=6_000_000_000, bytes_accessed=8_000_000, transcendentals=1_400_000),
    )(
        queries, residual, keys_values, out_weight, cache_weight,
        norm_gain[None, :], keep_rows[None, :], kept_count[None, :],
    )
    kept_cache = rotate_head(raw.astype(F32), positions).astype(BF)
    return (kept_hidden, kept_cache)


def solution(mesh):
    in_specs = (
        P("ctx", "tp"),
        P("ctx", "tp"),
        P("ctx", None),
        P("tp", "ctx"),
        P(),
        P(None, "tp"),
        P("ctx"),
        P("ctx"),
        P("ctx"),
    )
    out_specs = (P("ctx", "tp"), P("ctx", "tp"))
    fits = mesh.shape["ctx"] == 4 and mesh.shape["tp"] == 8
    body = fused_shards if fits else shards
    return jax.shard_map(body, mesh=mesh, in_specs=in_specs, out_specs=out_specs, check_vma=False)
```

```python
import math

import jax
import jax.numpy as jnp
from jax import lax
from jax.experimental import pallas as pl
from jax.experimental.pallas import tpu as pltpu
from jax.sharding import PartitionSpec as P

D = 8192
HQ = 64
KVH = 8
HD = 128


THETA = 1000000.0
EPS = 1e-06


def rotate_pairs(cache_rows, position_ids, first_col, head_dim):
    pair_count = cache_rows.shape[1] // 2
    columns = first_col + 2 * jnp.arange(pair_count, dtype=jnp.int32)
    within = columns % (2 * head_dim)
    is_key = within < head_dim
    exponent = jnp.where(is_key, within, 0).astype(jnp.float32) / head_dim
    frequency = jnp.power(jnp.float32(THETA), -exponent)
    angles = position_ids.astype(jnp.float32)[:, None] * frequency[None, :]
    paired = cache_rows.reshape(cache_rows.shape[0], pair_count, 2)
    first_half = paired[..., 0]
    second = paired[..., 1]
    cosine = jnp.cos(angles)
    sine_rows = jnp.sin(angles)
    turned_first = first_half * cosine - second * sine_rows
    turned_second = second * cosine + first_half * sine_rows
    turned = jnp.stack(
        [jnp.where(is_key, turned_first, first_half), jnp.where(is_key, turned_second, second)], -1
    )
    return turned.reshape(cache_rows.shape)


def shards(
    residual,
    queries,
    keys_values,
    out_weight,
    norm_gain,
    cache_weight,
    positions,
    keep_rows,
    kept_count,
):
    row_count = residual.shape[0]
    ctx_index = lax.axis_index("ctx")
    tp_index = lax.axis_index("tp")
    head_count = queries.shape[1] // HD
    kv_head = tp_index * head_count // (HQ // KVH)
    head_block = lax.dynamic_slice_in_dim(keys_values, kv_head * 2 * HD, 2 * HD, 1)
    key_rows = head_block[:, :HD]
    value_rows = head_block[:, HD:]
    query_rows = queries.reshape(row_count, head_count, HD)
    own_index = ctx_index * row_count + jnp.arange(row_count, dtype=jnp.int32)
    score_scale = 1.0 / math.sqrt(HD)
    running_max = jnp.full((row_count, head_count), -1e30, jnp.float32)
    key_block = lax.all_gather(key_rows, "ctx", axis=0, tiled=True)
    value_block = lax.all_gather(value_rows, "ctx", axis=0, tiled=True)
    block_rows = key_block.shape[0]
    scores = (
        jnp.einsum("rgd,kd->rgk", query_rows, key_block, preferred_element_type=jnp.float32)
        * score_scale
    )
    visible = jnp.arange(block_rows, dtype=jnp.int32)[None, :] <= own_index[:, None]
    visible = visible[:, None, :]
    scores = jnp.where(visible, scores, -1e30)
    new_max = jnp.maximum(running_max, jnp.max(scores, axis=-1))
    weights = jnp.where(visible, jnp.exp(scores - new_max[..., None]), 0.0)
    new_sum = jnp.sum(weights, axis=-1)
    update = jnp.einsum(
        "rgk,kd->rgd", weights.astype(jnp.bfloat16), value_block, preferred_element_type=jnp.float32
    )
    attended = (
        (update / new_sum[..., None]).reshape(row_count, head_count * HD).astype(jnp.bfloat16)
    )
    own_count = kept_count[0]
    valid_rows = jnp.arange(row_count, dtype=jnp.int32) < own_count
    partials = jnp.dot(
        attended,
        lax.all_gather(out_weight, "ctx", axis=1, tiled=True),
        preferred_element_type=jnp.float32,
    )
    group_sums = lax.psum_scatter(
        partials.astype(jnp.bfloat16), "tp", scatter_dimension=1, tiled=True
    ).astype(jnp.float32)
    hidden = (residual.astype(jnp.float32) + group_sums).astype(jnp.bfloat16)
    feat_width = hidden.shape[1]
    wide_hidden = hidden.astype(jnp.float32)
    square_total = lax.psum(jnp.sum(wide_hidden * wide_hidden, axis=-1), "tp")
    inverse = lax.rsqrt(square_total / D + EPS)
    gain_part = lax.dynamic_slice_in_dim(norm_gain, tp_index * feat_width, feat_width)
    normed = (wide_hidden * inverse[:, None] * gain_part[None, :]).astype(jnp.bfloat16)
    gathered = lax.all_gather(normed, "tp", axis=1, tiled=True)
    cache_rows = jnp.dot(gathered, cache_weight, preferred_element_type=jnp.float32)
    cache_rot = rotate_pairs(cache_rows, positions, tp_index * cache_rows.shape[1], HD).astype(
        jnp.bfloat16
    )
    kept_flags = jnp.zeros((row_count,), jnp.int32).at[keep_rows].set(valid_rows.astype(jnp.int32))
    kept_mask = kept_flags[:, None] > 0
    kept_hidden = jnp.where(kept_mask, hidden, jnp.zeros_like(hidden))
    kept_cache = jnp.where(kept_mask, cache_rot, jnp.zeros_like(cache_rot))
    return (kept_hidden, kept_cache)


KEPT = 160
Z = 4
MESH = pl.DeviceIdType.MESH
BF = jnp.bfloat16
F32 = jnp.float32


def fused_kernel(
    q_hbm, r_hbm, kv_hbm, w_hbm, cw_hbm, gain_hbm, keep_hbm, count_ref,
    hid_out, cache_out,
    gain_ref, keep_ref, q_ref, r_ref, kvbuf, w_ref, cw_ref, qown, qrecv, rown, rrecv, resbuf, attb, ownp, ysend, yrecv,
    zsum, zrecv, xrecv, hbuf, ymsg, ymsg_in, cmsg, crecv, cbuf, hpair,
    loc_sem, kv_s, kv_r, q_s, q_r, res_s, res_r, att_s, att_r, y_s, y_r, z_s, z_r, x_r,
    ag_s, ag_r, fw_s, ay_s, ay_r, cw_s, cw_r, c_s, c_r, row_s, row_r, fin_s, fin_r,
):
    c = lax.axis_index("ctx")
    t = lax.axis_index("tp")
    p, k = c // 2, c % 2
    z, y = t // 2, t % 2
    rows = q_ref.shape[0]
    near = z + 1 - 2 * (z % 2)
    cross = Z - 1 - z
    is_inner = (z + 1) // 2 == 1

    def ctx_peer(i):
        return ((p + i // 2) % 2) * 2 + (k + i % 2) % 2

    sib = ctx_peer(1)
    ydev = (c, 2 * z + 1 - y)
    is_root = c == z
    pending = []

    def remote(src, dst, ss, rs, dev):
        return pltpu.make_async_remote_copy(
            src_ref=src, dst_ref=dst, send_sem=ss, recv_sem=rs, device_id=dev, device_id_type=MESH
        )

    def send(src, dst, ss, rs, dev):
        copy = remote(src, dst, ss, rs, dev)
        copy.start()
        pending.append(copy)
        return copy

    feat = cw_ref.shape[1]
    own_kv = kvbuf.at[pl.ds(pl.multiple_of(c * rows, rows), rows)]
    kv_copy = pltpu.make_async_copy(
        kv_hbm.at[:, pl.ds(pl.multiple_of(t * 2 * HD, 2 * HD), 2 * HD)], own_kv, loc_sem.at[2]
    )
    kv_copy.start()
    keep_load = pltpu.make_async_copy(keep_hbm, keep_ref, loc_sem.at[5])
    keep_load.start()
    q_load = pltpu.make_async_copy(q_hbm, q_ref, loc_sem.at[3])
    q_load.start()
    r_load = pltpu.make_async_copy(r_hbm, r_ref, loc_sem.at[4])
    r_load.start()
    w_copy = pltpu.make_async_copy(w_hbm, w_ref, loc_sem.at[0])
    w_copy.start()
    first_feat = pl.multiple_of((2 * c + y) * feat, feat)
    cw_copy = pltpu.make_async_copy(cw_hbm.at[pl.ds(first_feat, feat)], cw_ref.at[0], loc_sem.at[1])
    cw_copy.start()

    gain_load = pltpu.make_async_copy(gain_hbm, gain_ref, loc_sem.at[6])
    gain_load.start()

    barrier = pltpu.get_barrier_semaphore()
    partners = [(ctx_peer(i), t) for i in (1, 2, 3)]
    partners += [(c, zz * 2 + y) for zz in (near, cross)] + [ydev]
    for dev in partners:
        pl.semaphore_signal(barrier, inc=1, device_id=dev, device_id_type=MESH)
    pl.semaphore_wait(barrier, len(partners))

    count = count_ref[...]
    keep_load.wait()
    base = jnp.where(k == 0, 0, 2 * KEPT - count)
    chosen = keep_ref[...] == lax.broadcasted_iota(jnp.int32, (rows, rows), 0)
    rank = lax.broadcasted_iota(jnp.int32, (rows, KEPT), 0)
    slot_at = lax.broadcasted_iota(jnp.int32, (rows, KEPT), 1)
    chosen = jnp.where(chosen, 1.0, 0.0).astype(BF)

    def place_of(kk):
        hit = (rank + base == slot_at + kk * KEPT) & (rank < count)
        return jnp.dot(
            chosen, jnp.where(hit, 1.0, 0.0).astype(BF), preferred_element_type=F32
        ).astype(BF)

    place_sib = place_of(1 - k)
    place_own = place_of(k)
    row_id = lax.broadcasted_iota(jnp.int32, (rows, HD), 0).astype(F32)
    lane = lax.broadcasted_iota(jnp.int32, (rows, HD), 1)
    tags = jnp.where(lane == 0, row_id, jnp.where(lane == 1, 1.0, 0.0)).astype(BF)
    width = q_ref.shape[1]

    def pick(sel, what):
        return lax.dot_general(
            sel, what, (((0,), (0,)), ((), ())), preferred_element_type=F32
        ).astype(BF)

    kv_copy.wait()
    kv_far = send(own_kv, own_kv, kv_s.at[0], kv_r.at[0], (ctx_peer(2), t))
    kv_sib = send(own_kv, own_kv, kv_s.at[1], kv_r.at[1], (sib, t))
    cw_send = send(
        cw_hbm.at[pl.ds(pl.multiple_of((2 * c + 1 - y) * feat, feat), feat)],
        cw_ref.at[1], cw_s, cw_r, ydev,
    )
    q_load.wait()
    qown[0, :, :width] = pick(place_sib, q_ref[...])
    qown[0, :, width:] = pick(place_sib, tags)
    q_copy = send(qown.at[0], qrecv, q_s.at[0], q_r.at[0], (sib, t))
    r_load.wait()
    rown[0] = pick(place_sib, r_ref[...])
    r_copy = send(rown.at[0], rrecv, q_s.at[1], q_r.at[1], (sib, t))
    qown[1, :, :width] = pick(place_own, q_ref[...])
    qown[1, :, width:] = pick(place_own, tags)
    rown[1] = pick(place_own, r_ref[...])

    kv_far.wait_recv()
    far_kv = kvbuf.at[pl.ds(pl.multiple_of(ctx_peer(2) * rows, rows), rows)]
    kv_diag = send(far_kv, far_kv, kv_s.at[2], kv_r.at[2], (sib, t))
    q_copy.wait_recv()
    own_tag = qown[1, :, width:].astype(F32)
    sib_tag = qrecv[:, width:].astype(F32)
    first_own = (c * rows).astype(F32)
    first_sib = (sib * rows).astype(F32)
    limit = (
        own_tag[:, 0:1] + first_own * own_tag[:, 1:2] + sib_tag[:, 0:1] + first_sib * sib_tag[:, 1:2]
    )
    qown[1, :, :width] = qown[1, :, :width] + qrecv[:, :width]

    r_copy.wait_recv()
    rown[1] = rown[1] + rrecv[...]
    res_slot = ((p + z // 2) % 2) * 2 + (k + z) % 2
    res_copy = remote(
        rown.at[1], resbuf.at[res_slot], res_s, res_r.at[res_slot], (z, t)
    )

    @pl.when(is_root)
    def _():
        resbuf[0] = rown[1]

    @pl.when(jnp.logical_not(is_root))
    def _():
        res_copy.start()

    kv_sib.wait_recv()
    kv_diag.wait_recv()
    total = kvbuf.shape[0]
    col_id = lax.broadcasted_iota(jnp.int32, (KEPT, total), 1).astype(F32)
    seen = col_id <= limit
    scale = 1.0 / math.sqrt(HD)
    keys = kvbuf[:, :HD]
    values = kvbuf[:, HD:]
    for h in range(width // HD):
        cols = slice(h * HD, (h + 1) * HD)
        s = lax.dot_general(
            qown[1, :, cols], keys, (((1,), (1,)), ((), ())), preferred_element_type=F32
        ) * scale
        s = jnp.where(seen, s, -1e30)
        top = jnp.max(s, axis=1, keepdims=True)
        e = jnp.exp(s - top)
        den = jnp.sum(e, axis=1, keepdims=True)
        mixed = jnp.dot(e.astype(BF), values, preferred_element_type=F32)
        attb[0, :, cols] = (mixed / den).astype(BF)

    att_cp = send(attb.at[0], attb.at[2], att_s.at[0], att_r.at[0], (ctx_peer(2), t))
    att_sib = send(attb.at[0], attb.at[1], att_s.at[1], att_r.at[1], (sib, t))
    half = Z * 256
    other = 2 * (1 - z // 2)
    mine = 2 - other
    is_outer = jnp.logical_not(is_inner)
    near_dev = (c, near * 2 + y)
    cross_dev = (c, cross * 2 + y)
    sequence = [(jj, other + jj) for jj in range(2)] + [(2 + jj, mine + jj) for jj in range(2)]

    def piece_of(who, j):
        return pl.ds(pl.multiple_of(who * half + j * 256, 256), 256)

    def y_copy(i, j):
        return remote(ysend.at[i, j], yrecv.at[i, j], y_s.at[i, j], y_r.at[i, j], ydev)

    def out_copy(i, j):
        return remote(zsum.at[i, j], zrecv.at[i, j], z_s.at[i, j], z_r.at[i, j], near_dev)

    def cross_copy(i, j):
        return remote(zsum.at[i, j], xrecv.at[i, j], z_s.at[i, j], x_r.at[i, j], cross_dev)
    w_copy.wait()
    fwd = {}
    ays, cs = {}, {}

    def stage_a(i):
        if i == 1:
            att_sib.wait_recv()
        if i == 2:
            att_cp.wait_recv()
            fwd[0] = send(attb.at[2], attb.at[3], att_s.at[2], att_r.at[2], (sib, t))
        if i == 3:
            fwd[0].wait_recv()
        for _, j in sequence:
            ysend[i, j] = jnp.dot(
                attb[i], w_ref[:, piece_of(1 - y, j)], preferred_element_type=F32
            ).astype(BF)
            copy = y_copy(i, j)
            copy.start()
            pending.append(copy)
        for _, j in sequence:
            ownp[i, j] = jnp.dot(
                attb[i], w_ref[:, piece_of(y, j)], preferred_element_type=F32
            )

    def stage_b(i):
        @pl.when(is_root)
        def _():
            if i > 0:
                remote(
                    rown.at[1], resbuf.at[i], res_s, res_r.at[i], (ctx_peer(i), t)
                ).wait_recv()
            for j in range(Z):
                ownp[i, j] = ownp[i, j] + resbuf[i, :, j * 256 : (j + 1) * 256].astype(F32)

        for _, j in sequence:
            y_copy(i, j).wait_recv()
            total = ownp[i, j] + yrecv[i, j].astype(F32)

            @pl.when(is_outer)
            def _():
                zsum[i, j] = total.astype(BF)
                out_copy(i, j).start()

            @pl.when(is_inner)
            def _():
                ownp[i, j] = total

    def stage_g(i):
        @pl.when(is_inner)
        def _():
            for n, j in sequence:
                out_copy(i, j).wait_recv()
                total = ownp[i, j] + zrecv[i, j].astype(F32)
                if n < 2:
                    zsum[i, j] = total.astype(BF)
                    cross_copy(i, j).start()
                else:
                    ownp[i, j] = total

    def piece_copy(i, j, dev, sem):
        piece = hbuf.at[i, j]
        return remote(piece, piece, sem.at[i, j], ag_r.at[i, j], dev)

    def stage_c(i):
        @pl.when(is_inner)
        def _():
            for n, j in sequence[2:]:
                cross_copy(i, j).wait_recv()
                hbuf[i, j] = (ownp[i, j] + xrecv[i, j].astype(F32)).astype(BF)
                piece_copy(i, j, cross_dev, ag_s).start()
                piece_copy(i, j, near_dev, fw_s).start()

    def stage_f(i):
        @pl.when(is_inner)
        def _():
            for n, j in sequence[:2]:
                piece_copy(i, j, cross_dev, ag_s).wait_recv()
                piece_copy(i, j, near_dev, fw_s).start()

    def row_copy(i):
        return remote(
            hbuf.at[i], hpair.at[(k + i % 2) % 2], row_s.at[i], row_r, (ctx_peer(i), t)
        )

    own_part = {}

    def packed(acc, squares):
        coarse = squares.astype(BF).astype(F32)
        at = lax.broadcasted_iota(jnp.int32, (KEPT, HD), 1)
        tail = jnp.where(at == 0, coarse, jnp.where(at == 1, squares - coarse, 0.0))
        return acc.astype(BF), tail.astype(BF)

    def unpacked(ref, i):
        tail = ref[i, :, 256:].astype(F32)
        return ref[i, :, :256].astype(F32), tail[:, 0:1] + tail[:, 1:2]

    def stage_d(i):
        @pl.when(is_outer)
        def _():
            for _, j in sequence[2:] + sequence[:2]:
                piece_copy(i, j, near_dev, fw_s).wait_recv()

        @pl.when(is_root)
        def _():
            if i == 0:
                hpair[k] = hbuf[i]
            else:
                row_copy(i).start()

        if i == 0:
            gain_load.wait()
            cw_copy.wait()
            cw_send.wait_recv()
        far = jnp.zeros((KEPT, 256), F32)
        acc = jnp.zeros((KEPT, 256), F32)
        squares = jnp.zeros((KEPT, 1), F32)
        for q in range(Z):
            wide = hbuf[i, q].astype(F32)
            squares = squares + jnp.sum(wide * wide, axis=1, keepdims=True)
            gain = gain_ref[:, pl.ds(pl.multiple_of(first_feat + q * 256, 256), 256)]
            scaled = (wide * gain).astype(BF)
            cut = slice(q * 256, (q + 1) * 256)
            far = far + jnp.dot(scaled, cw_ref[1, cut], preferred_element_type=F32)
            acc = acc + jnp.dot(scaled, cw_ref[0, cut], preferred_element_type=F32)
        ymsg[i, :, :256], ymsg[i, :, 256:] = packed(far, squares)
        ays[i] = send(ymsg.at[i], ymsg_in.at[i], ay_s.at[i], ay_r.at[i], ydev)
        own_part[i] = acc, squares

    def stage_e(i):
        ays[i].wait_recv()
        acc, squares = own_part[i]
        more, more_squares = unpacked(ymsg_in, i)
        acc = acc + more
        squares = squares + more_squares
        if i == 0:
            return acc, squares
        cmsg[i - 1, :, :256], cmsg[i - 1, :, 256:] = packed(acc, squares)
        cs[i] = send(
            cmsg.at[i - 1], crecv.at[i - 1], c_s.at[i - 1], c_r.at[i - 1], (ctx_peer(i), t)
        )
        return None

    stage_a(0)
    stage_a(1)
    stage_b(0)
    stage_a(2)
    stage_b(1)
    stage_g(0)
    stage_a(3)
    stage_b(2)
    stage_g(1)
    stage_c(0)
    stage_b(3)
    stage_g(2)
    stage_c(1)
    stage_f(0)
    stage_g(3)
    stage_c(2)
    stage_f(1)
    stage_d(0)
    stage_c(3)
    stage_f(2)
    stage_d(1)
    stage_f(3)
    stage_d(2)
    stage_e(1)
    stage_d(3)
    stage_e(2)

    @pl.when(jnp.logical_not(is_root))
    def _():
        row_copy(1).wait_recv()

    pair_copy = send(hpair.at[k], hpair.at[k], fin_s.at[0], fin_r.at[0], (sib, t))
    stage_e(3)
    acc, squares = stage_e(0)
    place = [place_of(kk) for kk in range(2)]
    pair_copy.wait_recv()
    for j in range(Z):
        hid_out[:, j * 256 : (j + 1) * 256] = (
            jnp.dot(place[0], hpair[0, j], preferred_element_type=F32)
            + jnp.dot(place[1], hpair[1, j], preferred_element_type=F32)
        ).astype(BF)
    for i in (1, 2, 3):
        cs[i].wait_recv()
        more, more_squares = unpacked(crecv, i - 1)
        acc = acc + more
        squares = squares + more_squares
    cbuf[k] = (acc * lax.rsqrt(squares / D + EPS)).astype(BF)
    last = send(cbuf.at[k], cbuf.at[k], fin_s.at[1], fin_r.at[1], (sib, t))
    last.wait_recv()
    cache_out[...] = (
        jnp.dot(place[0], cbuf[0], preferred_element_type=F32)
        + jnp.dot(place[1], cbuf[1], preferred_element_type=F32)
    ).astype(BF)

    for copy in pending:
        copy.wait_send()

    @pl.when(jnp.logical_not(is_root))
    def _():
        res_copy.wait_send()

    @pl.when(is_root)
    def _():
        for i in (1, 2, 3):
            row_copy(i).wait_send()

    @pl.when(is_inner)
    def _():
        for i in range(4):
            for n, j in sequence:
                piece_copy(i, j, near_dev, fw_s).wait_send()
                if n < 2:
                    cross_copy(i, j).wait_send()
                else:
                    piece_copy(i, j, cross_dev, ag_s).wait_send()

    @pl.when(is_outer)
    def _():
        for i in range(4):
            for _, j in sequence:
                out_copy(i, j).wait_send()


def rotate_head(raw, position_ids):
    column = jnp.arange(raw.shape[1], dtype=jnp.int32)
    within = column - column % 2
    is_key = column < HD
    exponent = jnp.where(is_key, within, 0).astype(F32) / HD
    frequency = jnp.power(jnp.float32(THETA), -exponent)
    angles = position_ids.astype(F32)[:, None] * frequency[None, :]
    cosine = jnp.where(is_key, jnp.cos(angles), 1.0)
    sine = jnp.where(is_key, jnp.sin(angles), 0.0)
    partner = jnp.where(column % 2 == 0, -jnp.roll(raw, -1, axis=1), jnp.roll(raw, 1, axis=1))
    return raw * cosine + partner * sine


def fused_shards(
    residual, queries, keys_values, out_weight, norm_gain, cache_weight, positions, keep_rows, kept_count
):
    rows, width = queries.shape
    feat = out_weight.shape[1]
    n_ctx = D // feat
    dma = pltpu.SemaphoreType.DMA
    vmem = pl.BlockSpec(memory_space=pltpu.VMEM)
    hbm = pl.BlockSpec(memory_space=pl.ANY)
    kept_hidden, raw = pl.pallas_call(
        fused_kernel,
        out_shape=(
            jax.ShapeDtypeStruct((rows, width), BF),
            jax.ShapeDtypeStruct((rows, 2 * HD), BF),
        ),
        in_specs=[hbm] * 7 + [vmem],
        out_specs=(vmem, vmem),
        scratch_shapes=[
            pltpu.VMEM((1, D), F32),
            pltpu.VMEM((1, rows), jnp.int32),
            pltpu.VMEM((rows, width), BF),
            pltpu.VMEM((rows, width), BF),
            pltpu.VMEM((n_ctx * rows, 2 * HD), BF),
            pltpu.VMEM(out_weight.shape, BF),
            pltpu.VMEM((2, feat // 2, 2 * HD), BF),
            pltpu.VMEM((2, KEPT, width + HD), BF),
            pltpu.VMEM((KEPT, width + HD), BF),
            pltpu.VMEM((2, KEPT, width), BF),
            pltpu.VMEM((KEPT, width), BF),
            pltpu.VMEM((4, KEPT, width), BF),
            pltpu.VMEM((4, KEPT, width), BF),
            pltpu.VMEM((4, Z, KEPT, 256), F32),
            pltpu.VMEM((4, Z, KEPT, 256), BF),
            pltpu.VMEM((4, Z, KEPT, 256), BF),
            pltpu.VMEM((4, Z, KEPT, 256), BF),
            pltpu.VMEM((4, Z, KEPT, 256), BF),
            pltpu.VMEM((4, Z, KEPT, 256), BF),
            pltpu.VMEM((4, Z, KEPT, 256), BF),
            pltpu.VMEM((4, KEPT, 256 + HD), BF),
            pltpu.VMEM((4, KEPT, 256 + HD), BF),
            pltpu.VMEM((3, KEPT, 256 + HD), BF),
            pltpu.VMEM((3, KEPT, 256 + HD), BF),
            pltpu.VMEM((2, KEPT, 256), BF),
            pltpu.VMEM((2, Z, KEPT, 256), BF),
            dma((7,)), dma((3,)), dma((3,)), dma((2,)), dma((2,)), dma, dma((4,)),
            dma((3,)), dma((3,)), dma((4, 4)), dma((4, 4)), dma((4, 4)), dma((4, 4)), dma((4, 4)),
            dma((4, 4)), dma((4, 4)), dma((4, 4)), dma((4,)), dma((4,)), dma, dma, dma((3,)), dma((3,)),
            dma((4,)), dma, dma((2,)), dma((2,)),
        ],
        compiler_params=pltpu.CompilerParams(
            collective_id=0, has_side_effects=True, vmem_limit_bytes=60 * 1024 * 1024
        ),
        cost_estimate=pl.CostEstimate(flops=6_000_000_000, bytes_accessed=8_000_000, transcendentals=1_400_000),
    )(
        queries, residual, keys_values, out_weight, cache_weight,
        norm_gain[None, :], keep_rows[None, :], kept_count[None, :],
    )
    kept_cache = rotate_head(raw.astype(F32), positions).astype(BF)
    return (kept_hidden, kept_cache)


def solution(mesh):
    in_specs = (
        P("ctx", "tp"),
        P("ctx", "tp"),
        P("ctx", None),
        P("tp", "ctx"),
        P(),
        P(None, "tp"),
        P("ctx"),
        P("ctx"),
        P("ctx"),
    )
    out_specs = (P("ctx", "tp"), P("ctx", "tp"))
    fits = mesh.shape["ctx"] == 4 and mesh.shape["tp"] == 8
    body = fused_shards if fits else shards
    return jax.shard_map(body, mesh=mesh, in_specs=in_specs, out_specs=out_specs, check_vma=False)
```

```python
import math

import jax
import jax.numpy as jnp
from jax import lax
from jax.experimental import pallas as pl
from jax.experimental.pallas import tpu as pltpu
from jax.sharding import PartitionSpec as P

D = 8192
HQ = 64
KVH = 8
HD = 128


THETA = 1000000.0
EPS = 1e-06


def rotate_pairs(cache_rows, position_ids, first_col, head_dim):
    pair_count = cache_rows.shape[1] // 2
    columns = first_col + 2 * jnp.arange(pair_count, dtype=jnp.int32)
    within = columns % (2 * head_dim)
    is_key = within < head_dim
    exponent = jnp.where(is_key, within, 0).astype(jnp.float32) / head_dim
    frequency = jnp.power(jnp.float32(THETA), -exponent)
    angles = position_ids.astype(jnp.float32)[:, None] * frequency[None, :]
    paired = cache_rows.reshape(cache_rows.shape[0], pair_count, 2)
    first_half = paired[..., 0]
    second = paired[..., 1]
    cosine = jnp.cos(angles)
    sine_rows = jnp.sin(angles)
    turned_first = first_half * cosine - second * sine_rows
    turned_second = second * cosine + first_half * sine_rows
    turned = jnp.stack(
        [jnp.where(is_key, turned_first, first_half), jnp.where(is_key, turned_second, second)], -1
    )
    return turned.reshape(cache_rows.shape)


def shards(
    residual,
    queries,
    keys_values,
    out_weight,
    norm_gain,
    cache_weight,
    positions,
    keep_rows,
    kept_count,
):
    row_count = residual.shape[0]
    ctx_index = lax.axis_index("ctx")
    tp_index = lax.axis_index("tp")
    head_count = queries.shape[1] // HD
    kv_head = tp_index * head_count // (HQ // KVH)
    head_block = lax.dynamic_slice_in_dim(keys_values, kv_head * 2 * HD, 2 * HD, 1)
    key_rows = head_block[:, :HD]
    value_rows = head_block[:, HD:]
    query_rows = queries.reshape(row_count, head_count, HD)
    own_index = ctx_index * row_count + jnp.arange(row_count, dtype=jnp.int32)
    score_scale = 1.0 / math.sqrt(HD)
    running_max = jnp.full((row_count, head_count), -1e30, jnp.float32)
    key_block = lax.all_gather(key_rows, "ctx", axis=0, tiled=True)
    value_block = lax.all_gather(value_rows, "ctx", axis=0, tiled=True)
    block_rows = key_block.shape[0]
    scores = (
        jnp.einsum("rgd,kd->rgk", query_rows, key_block, preferred_element_type=jnp.float32)
        * score_scale
    )
    visible = jnp.arange(block_rows, dtype=jnp.int32)[None, :] <= own_index[:, None]
    visible = visible[:, None, :]
    scores = jnp.where(visible, scores, -1e30)
    new_max = jnp.maximum(running_max, jnp.max(scores, axis=-1))
    weights = jnp.where(visible, jnp.exp(scores - new_max[..., None]), 0.0)
    new_sum = jnp.sum(weights, axis=-1)
    update = jnp.einsum(
        "rgk,kd->rgd", weights.astype(jnp.bfloat16), value_block, preferred_element_type=jnp.float32
    )
    attended = (
        (update / new_sum[..., None]).reshape(row_count, head_count * HD).astype(jnp.bfloat16)
    )
    own_count = kept_count[0]
    valid_rows = jnp.arange(row_count, dtype=jnp.int32) < own_count
    partials = jnp.dot(
        attended,
        lax.all_gather(out_weight, "ctx", axis=1, tiled=True),
        preferred_element_type=jnp.float32,
    )
    group_sums = lax.psum_scatter(
        partials.astype(jnp.bfloat16), "tp", scatter_dimension=1, tiled=True
    ).astype(jnp.float32)
    hidden = (residual.astype(jnp.float32) + group_sums).astype(jnp.bfloat16)
    feat_width = hidden.shape[1]
    wide_hidden = hidden.astype(jnp.float32)
    square_total = lax.psum(jnp.sum(wide_hidden * wide_hidden, axis=-1), "tp")
    inverse = lax.rsqrt(square_total / D + EPS)
    gain_part = lax.dynamic_slice_in_dim(norm_gain, tp_index * feat_width, feat_width)
    normed = (wide_hidden * inverse[:, None] * gain_part[None, :]).astype(jnp.bfloat16)
    gathered = lax.all_gather(normed, "tp", axis=1, tiled=True)
    cache_rows = jnp.dot(gathered, cache_weight, preferred_element_type=jnp.float32)
    cache_rot = rotate_pairs(cache_rows, positions, tp_index * cache_rows.shape[1], HD).astype(
        jnp.bfloat16
    )
    kept_flags = jnp.zeros((row_count,), jnp.int32).at[keep_rows].set(valid_rows.astype(jnp.int32))
    kept_mask = kept_flags[:, None] > 0
    kept_hidden = jnp.where(kept_mask, hidden, jnp.zeros_like(hidden))
    kept_cache = jnp.where(kept_mask, cache_rot, jnp.zeros_like(cache_rot))
    return (kept_hidden, kept_cache)


KEPT = 160
Z = 4
MESH = pl.DeviceIdType.MESH
BF = jnp.bfloat16
F32 = jnp.float32


def fused_kernel(
    q_hbm, r_hbm, kv_hbm, w_hbm, cw_hbm, gain_hbm, keep_hbm, count_ref,
    hid_out, cache_out,
    gain_ref, keep_ref, q_ref, r_ref, kvbuf, w_ref, cw_ref, qown, qrecv, rown, rrecv, resbuf, attb, ownp, ysend, yrecv,
    zsum, zrecv, xrecv, hbuf, ymsg, ymsg_in, cmsg, crecv, cbuf, hpair,
    loc_sem, kv_s, kv_r, q_s, q_r, res_s, res_r, att_s, att_r, y_s, y_r, z_s, z_r, x_r,
    ag_s, ag_r, fw_s, ay_s, ay_r, cw_s, cw_r, c_s, c_r, row_s, row_r, fin_s, fin_r,
):
    c = lax.axis_index("ctx")
    t = lax.axis_index("tp")
    p, k = c // 2, c % 2
    z, y = t // 2, t % 2
    rows = q_ref.shape[0]
    near = z + 1 - 2 * (z % 2)
    cross = Z - 1 - z
    is_inner = (z + 1) // 2 == 1

    def ctx_peer(i):
        return ((p + i // 2) % 2) * 2 + (k + i % 2) % 2

    sib = ctx_peer(1)
    ydev = (c, 2 * z + 1 - y)
    is_root = c == z
    pending = []

    def remote(src, dst, ss, rs, dev):
        return pltpu.make_async_remote_copy(
            src_ref=src, dst_ref=dst, send_sem=ss, recv_sem=rs, device_id=dev, device_id_type=MESH
        )

    def send(src, dst, ss, rs, dev):
        copy = remote(src, dst, ss, rs, dev)
        copy.start()
        pending.append(copy)
        return copy

    feat = cw_ref.shape[1]
    own_kv = kvbuf.at[pl.ds(pl.multiple_of(c * rows, rows), rows)]
    kv_copy = pltpu.make_async_copy(
        kv_hbm.at[:, pl.ds(pl.multiple_of(t * 2 * HD, 2 * HD), 2 * HD)], own_kv, loc_sem.at[2]
    )
    kv_copy.start()
    keep_load = pltpu.make_async_copy(keep_hbm, keep_ref, loc_sem.at[5])
    keep_load.start()
    q_load = pltpu.make_async_copy(q_hbm, q_ref, loc_sem.at[3])
    q_load.start()
    r_load = pltpu.make_async_copy(r_hbm, r_ref, loc_sem.at[4])
    r_load.start()
    w_copy = pltpu.make_async_copy(w_hbm, w_ref, loc_sem.at[0])
    w_copy.start()
    first_feat = pl.multiple_of((2 * c + y) * feat, feat)
    cw_copy = pltpu.make_async_copy(cw_hbm.at[pl.ds(first_feat, feat)], cw_ref.at[0], loc_sem.at[1])
    cw_copy.start()

    gain_load = pltpu.make_async_copy(gain_hbm, gain_ref, loc_sem.at[6])
    gain_load.start()

    barrier = pltpu.get_barrier_semaphore()
    partners = [(ctx_peer(i), t) for i in (1, 2, 3)]
    partners += [(c, zz * 2 + y) for zz in (near, cross)] + [ydev]
    for dev in partners:
        pl.semaphore_signal(barrier, inc=1, device_id=dev, device_id_type=MESH)
    pl.semaphore_wait(barrier, len(partners))

    count = count_ref[...]
    keep_load.wait()
    base = jnp.where(k == 0, 0, 2 * KEPT - count)
    chosen = keep_ref[...] == lax.broadcasted_iota(jnp.int32, (rows, rows), 0)
    rank = lax.broadcasted_iota(jnp.int32, (rows, KEPT), 0)
    slot_at = lax.broadcasted_iota(jnp.int32, (rows, KEPT), 1)
    chosen = jnp.where(chosen, 1.0, 0.0).astype(BF)

    def place_of(kk):
        hit = (rank + base == slot_at + kk * KEPT) & (rank < count)
        return jnp.dot(
            chosen, jnp.where(hit, 1.0, 0.0).astype(BF), preferred_element_type=F32
        ).astype(BF)

    place_sib = place_of(1 - k)
    place_own = place_of(k)
    row_id = lax.broadcasted_iota(jnp.int32, (rows, HD), 0).astype(F32)
    lane = lax.broadcasted_iota(jnp.int32, (rows, HD), 1)
    tags = jnp.where(lane == 0, row_id, jnp.where(lane == 1, 1.0, 0.0)).astype(BF)
    width = q_ref.shape[1]

    def pick(sel, what):
        return lax.dot_general(
            sel, what, (((0,), (0,)), ((), ())), preferred_element_type=F32
        ).astype(BF)

    kv_copy.wait()
    kv_far = send(own_kv, own_kv, kv_s.at[0], kv_r.at[0], (ctx_peer(2), t))
    kv_sib = send(own_kv, own_kv, kv_s.at[1], kv_r.at[1], (sib, t))
    cw_send = send(
        cw_hbm.at[pl.ds(pl.multiple_of((2 * c + 1 - y) * feat, feat), feat)],
        cw_ref.at[1], cw_s, cw_r, ydev,
    )
    q_load.wait()
    qown[0, :, :width] = pick(place_sib, q_ref[...])
    qown[0, :, width:] = pick(place_sib, tags)
    q_copy = send(qown.at[0], qrecv, q_s.at[0], q_r.at[0], (sib, t))
    r_load.wait()
    rown[0] = pick(place_sib, r_ref[...])
    r_copy = send(rown.at[0], rrecv, q_s.at[1], q_r.at[1], (sib, t))
    qown[1, :, :width] = pick(place_own, q_ref[...])
    qown[1, :, width:] = pick(place_own, tags)
    rown[1] = pick(place_own, r_ref[...])

    kv_far.wait_recv()
    far_kv = kvbuf.at[pl.ds(pl.multiple_of(ctx_peer(2) * rows, rows), rows)]
    kv_diag = send(far_kv, far_kv, kv_s.at[2], kv_r.at[2], (sib, t))
    q_copy.wait_recv()
    own_tag = qown[1, :, width:].astype(F32)
    sib_tag = qrecv[:, width:].astype(F32)
    first_own = (c * rows).astype(F32)
    first_sib = (sib * rows).astype(F32)
    limit = (
        own_tag[:, 0:1] + first_own * own_tag[:, 1:2] + sib_tag[:, 0:1] + first_sib * sib_tag[:, 1:2]
    )
    qown[1, :, :width] = qown[1, :, :width] + qrecv[:, :width]

    r_copy.wait_recv()
    rown[1] = rown[1] + rrecv[...]
    res_slot = ((p + z // 2) % 2) * 2 + (k + z) % 2
    res_copy = remote(
        rown.at[1], resbuf.at[res_slot], res_s, res_r.at[res_slot], (z, t)
    )

    @pl.when(is_root)
    def _():
        resbuf[0] = rown[1]

    @pl.when(jnp.logical_not(is_root))
    def _():
        res_copy.start()

    kv_sib.wait_recv()
    kv_diag.wait_recv()
    total = kvbuf.shape[0]
    col_id = lax.broadcasted_iota(jnp.int32, (KEPT, total), 1).astype(F32)
    group = 4
    seen = col_id <= limit
    seen = jnp.concatenate([seen] * group, axis=0)
    scale = math.log2(math.e) / math.sqrt(HD)
    keys = kvbuf[:, :HD]
    values = kvbuf[:, HD:]
    for first in range(0, width // HD, group):
        heads = [slice(h * HD, (h + 1) * HD) for h in range(first, first + group)]
        s = lax.dot_general(
            jnp.concatenate([qown[1, :, cols] for cols in heads], axis=0),
            keys,
            (((1,), (1,)), ((), ())),
            preferred_element_type=F32,
        )
        s = jnp.where(seen, s, -1e30)
        top = jnp.max(s, axis=1, keepdims=True)
        e = jnp.exp2((s - top) * scale)
        den = jnp.sum(e, axis=1, keepdims=True)
        mixed = jnp.dot(e.astype(BF), values, preferred_element_type=F32) / den
        for n, cols in enumerate(heads):
            attb[0, :, cols] = mixed[n * KEPT : (n + 1) * KEPT].astype(BF)

    att_cp = send(attb.at[0], attb.at[2], att_s.at[0], att_r.at[0], (ctx_peer(2), t))
    att_sib = send(attb.at[0], attb.at[1], att_s.at[1], att_r.at[1], (sib, t))
    half = Z * 256
    other = 2 * (1 - z // 2)
    mine = 2 - other
    is_outer = jnp.logical_not(is_inner)
    near_dev = (c, near * 2 + y)
    cross_dev = (c, cross * 2 + y)
    sequence = [(jj, other + jj) for jj in range(2)] + [(2 + jj, mine + jj) for jj in range(2)]

    def piece_of(who, j):
        return pl.ds(pl.multiple_of(who * half + j * 256, 256), 256)

    def y_copy(i, j):
        return remote(ysend.at[i, j], yrecv.at[i, j], y_s.at[i, j], y_r.at[i, j], ydev)

    def out_copy(i, j):
        return remote(zsum.at[i, j], zrecv.at[i, j], z_s.at[i, j], z_r.at[i, j], near_dev)

    def cross_copy(i, j):
        return remote(zsum.at[i, j], xrecv.at[i, j], z_s.at[i, j], x_r.at[i, j], cross_dev)
    w_copy.wait()
    fwd = {}
    ays, cs = {}, {}

    def stage_a(i):
        if i == 1:
            att_sib.wait_recv()
        if i == 2:
            att_cp.wait_recv()
            fwd[0] = send(attb.at[2], attb.at[3], att_s.at[2], att_r.at[2], (sib, t))
        if i == 3:
            fwd[0].wait_recv()
        for _, j in sequence:
            ysend[i, j] = jnp.dot(
                attb[i], w_ref[:, piece_of(1 - y, j)], preferred_element_type=F32
            ).astype(BF)
            copy = y_copy(i, j)
            copy.start()
            pending.append(copy)
        for _, j in sequence:
            ownp[i, j] = jnp.dot(
                attb[i], w_ref[:, piece_of(y, j)], preferred_element_type=F32
            )

    def stage_b(i):
        @pl.when(is_root)
        def _():
            if i > 0:
                remote(
                    rown.at[1], resbuf.at[i], res_s, res_r.at[i], (ctx_peer(i), t)
                ).wait_recv()
            for j in range(Z):
                ownp[i, j] = ownp[i, j] + resbuf[i, :, j * 256 : (j + 1) * 256].astype(F32)

        for _, j in sequence:
            y_copy(i, j).wait_recv()
            total = ownp[i, j] + yrecv[i, j].astype(F32)

            @pl.when(is_outer)
            def _():
                zsum[i, j] = total.astype(BF)
                out_copy(i, j).start()

            @pl.when(is_inner)
            def _():
                ownp[i, j] = total

    def stage_g(i):
        @pl.when(is_inner)
        def _():
            for n, j in sequence:
                out_copy(i, j).wait_recv()
                total = ownp[i, j] + zrecv[i, j].astype(F32)
                if n < 2:
                    zsum[i, j] = total.astype(BF)
                    cross_copy(i, j).start()
                else:
                    ownp[i, j] = total

    def piece_copy(i, j, dev, sem):
        piece = hbuf.at[i, j]
        return remote(piece, piece, sem.at[i, j], ag_r.at[i, j], dev)

    def stage_c(i):
        @pl.when(is_inner)
        def _():
            for n, j in sequence[2:]:
                cross_copy(i, j).wait_recv()
                hbuf[i, j] = (ownp[i, j] + xrecv[i, j].astype(F32)).astype(BF)
                piece_copy(i, j, cross_dev, ag_s).start()
                piece_copy(i, j, near_dev, fw_s).start()

    def stage_f(i):
        @pl.when(is_inner)
        def _():
            for n, j in sequence[:2]:
                piece_copy(i, j, cross_dev, ag_s).wait_recv()
                piece_copy(i, j, near_dev, fw_s).start()

    def row_copy(i):
        return remote(
            hbuf.at[i], hpair.at[(k + i % 2) % 2], row_s.at[i], row_r, (ctx_peer(i), t)
        )

    own_part = {}

    def packed(acc, squares):
        coarse = squares.astype(BF).astype(F32)
        at = lax.broadcasted_iota(jnp.int32, (KEPT, HD), 1)
        tail = jnp.where(at == 0, coarse, jnp.where(at == 1, squares - coarse, 0.0))
        return acc.astype(BF), tail.astype(BF)

    def unpacked(ref, i):
        tail = ref[i, :, 256:].astype(F32)
        return ref[i, :, :256].astype(F32), tail[:, 0:1] + tail[:, 1:2]

    def stage_d(i):
        @pl.when(is_outer)
        def _():
            for _, j in sequence[2:] + sequence[:2]:
                piece_copy(i, j, near_dev, fw_s).wait_recv()

        @pl.when(is_root)
        def _():
            if i == 0:
                hpair[k] = hbuf[i]
            else:
                row_copy(i).start()

        if i == 0:
            gain_load.wait()
            cw_copy.wait()
            cw_send.wait_recv()
        far = jnp.zeros((KEPT, 256), F32)
        acc = jnp.zeros((KEPT, 256), F32)
        squares = jnp.zeros((KEPT, 1), F32)
        for q in range(Z):
            wide = hbuf[i, q].astype(F32)
            squares = squares + jnp.sum(wide * wide, axis=1, keepdims=True)
            gain = gain_ref[:, pl.ds(pl.multiple_of(first_feat + q * 256, 256), 256)]
            scaled = (wide * gain).astype(BF)
            cut = slice(q * 256, (q + 1) * 256)
            far = far + jnp.dot(scaled, cw_ref[1, cut], preferred_element_type=F32)
            acc = acc + jnp.dot(scaled, cw_ref[0, cut], preferred_element_type=F32)
        ymsg[i, :, :256], ymsg[i, :, 256:] = packed(far, squares)
        ays[i] = send(ymsg.at[i], ymsg_in.at[i], ay_s.at[i], ay_r.at[i], ydev)
        own_part[i] = acc, squares

    def stage_e(i):
        ays[i].wait_recv()
        acc, squares = own_part[i]
        more, more_squares = unpacked(ymsg_in, i)
        acc = acc + more
        squares = squares + more_squares
        if i == 0:
            return acc, squares
        cmsg[i - 1, :, :256], cmsg[i - 1, :, 256:] = packed(acc, squares)
        cs[i] = send(
            cmsg.at[i - 1], crecv.at[i - 1], c_s.at[i - 1], c_r.at[i - 1], (ctx_peer(i), t)
        )
        return None

    stage_a(0)
    stage_a(1)
    stage_b(0)
    stage_a(2)
    stage_g(0)
    stage_c(0)
    stage_b(1)
    stage_a(3)
    stage_f(0)
    stage_g(1)
    stage_d(0)
    stage_c(1)
    stage_b(2)
    stage_f(1)
    stage_g(2)
    stage_d(1)
    stage_c(2)
    stage_b(3)
    stage_f(2)
    stage_g(3)
    stage_e(1)
    stage_d(2)
    stage_c(3)
    stage_f(3)
    stage_e(2)
    stage_d(3)

    @pl.when(jnp.logical_not(is_root))
    def _():
        row_copy(1).wait_recv()

    pair_copy = send(hpair.at[k], hpair.at[k], fin_s.at[0], fin_r.at[0], (sib, t))
    stage_e(3)
    acc, squares = stage_e(0)
    place = [place_of(kk) for kk in range(2)]
    pair_copy.wait_recv()
    for j in range(Z):
        hid_out[:, j * 256 : (j + 1) * 256] = (
            jnp.dot(place[0], hpair[0, j], preferred_element_type=F32)
            + jnp.dot(place[1], hpair[1, j], preferred_element_type=F32)
        ).astype(BF)
    for i in (1, 2, 3):
        cs[i].wait_recv()
        more, more_squares = unpacked(crecv, i - 1)
        acc = acc + more
        squares = squares + more_squares
    cbuf[k] = (acc * lax.rsqrt(squares / D + EPS)).astype(BF)
    last = send(cbuf.at[k], cbuf.at[k], fin_s.at[1], fin_r.at[1], (sib, t))
    last.wait_recv()
    cache_out[...] = (
        jnp.dot(place[0], cbuf[0], preferred_element_type=F32)
        + jnp.dot(place[1], cbuf[1], preferred_element_type=F32)
    ).astype(BF)

    for copy in pending:
        copy.wait_send()

    @pl.when(jnp.logical_not(is_root))
    def _():
        res_copy.wait_send()

    @pl.when(is_root)
    def _():
        for i in (1, 2, 3):
            row_copy(i).wait_send()

    @pl.when(is_inner)
    def _():
        for i in range(4):
            for n, j in sequence:
                piece_copy(i, j, near_dev, fw_s).wait_send()
                if n < 2:
                    cross_copy(i, j).wait_send()
                else:
                    piece_copy(i, j, cross_dev, ag_s).wait_send()

    @pl.when(is_outer)
    def _():
        for i in range(4):
            for _, j in sequence:
                out_copy(i, j).wait_send()


def rotate_head(raw, position_ids):
    column = jnp.arange(raw.shape[1], dtype=jnp.int32)
    within = column - column % 2
    is_key = column < HD
    exponent = jnp.where(is_key, within, 0).astype(F32) / HD
    frequency = jnp.power(jnp.float32(THETA), -exponent)
    angles = position_ids.astype(F32)[:, None] * frequency[None, :]
    cosine = jnp.where(is_key, jnp.cos(angles), 1.0)
    sine = jnp.where(is_key, jnp.sin(angles), 0.0)
    partner = jnp.where(column % 2 == 0, -jnp.roll(raw, -1, axis=1), jnp.roll(raw, 1, axis=1))
    return raw * cosine + partner * sine


def fused_shards(
    residual, queries, keys_values, out_weight, norm_gain, cache_weight, positions, keep_rows, kept_count
):
    rows, width = queries.shape
    feat = out_weight.shape[1]
    n_ctx = D // feat
    dma = pltpu.SemaphoreType.DMA
    vmem = pl.BlockSpec(memory_space=pltpu.VMEM)
    hbm = pl.BlockSpec(memory_space=pl.ANY)
    kept_hidden, raw = pl.pallas_call(
        fused_kernel,
        out_shape=(
            jax.ShapeDtypeStruct((rows, width), BF),
            jax.ShapeDtypeStruct((rows, 2 * HD), BF),
        ),
        in_specs=[hbm] * 7 + [vmem],
        out_specs=(vmem, vmem),
        scratch_shapes=[
            pltpu.VMEM((1, D), F32),
            pltpu.VMEM((1, rows), jnp.int32),
            pltpu.VMEM((rows, width), BF),
            pltpu.VMEM((rows, width), BF),
            pltpu.VMEM((n_ctx * rows, 2 * HD), BF),
            pltpu.VMEM(out_weight.shape, BF),
            pltpu.VMEM((2, feat // 2, 2 * HD), BF),
            pltpu.VMEM((2, KEPT, width + HD), BF),
            pltpu.VMEM((KEPT, width + HD), BF),
            pltpu.VMEM((2, KEPT, width), BF),
            pltpu.VMEM((KEPT, width), BF),
            pltpu.VMEM((4, KEPT, width), BF),
            pltpu.VMEM((4, KEPT, width), BF),
            pltpu.VMEM((4, Z, KEPT, 256), F32),
            pltpu.VMEM((4, Z, KEPT, 256), BF),
            pltpu.VMEM((4, Z, KEPT, 256), BF),
            pltpu.VMEM((4, Z, KEPT, 256), BF),
            pltpu.VMEM((4, Z, KEPT, 256), BF),
            pltpu.VMEM((4, Z, KEPT, 256), BF),
            pltpu.VMEM((4, Z, KEPT, 256), BF),
            pltpu.VMEM((4, KEPT, 256 + HD), BF),
            pltpu.VMEM((4, KEPT, 256 + HD), BF),
            pltpu.VMEM((3, KEPT, 256 + HD), BF),
            pltpu.VMEM((3, KEPT, 256 + HD), BF),
            pltpu.VMEM((2, KEPT, 256), BF),
            pltpu.VMEM((2, Z, KEPT, 256), BF),
            dma((7,)), dma((3,)), dma((3,)), dma((2,)), dma((2,)), dma, dma((4,)),
            dma((3,)), dma((3,)), dma((4, 4)), dma((4, 4)), dma((4, 4)), dma((4, 4)), dma((4, 4)),
            dma((4, 4)), dma((4, 4)), dma((4, 4)), dma((4,)), dma((4,)), dma, dma, dma((3,)), dma((3,)),
            dma((4,)), dma, dma((2,)), dma((2,)),
        ],
        compiler_params=pltpu.CompilerParams(
            collective_id=0, has_side_effects=True, vmem_limit_bytes=60 * 1024 * 1024
        ),
        cost_estimate=pl.CostEstimate(flops=6_000_000_000, bytes_accessed=8_000_000, transcendentals=1_400_000),
    )(
        queries, residual, keys_values, out_weight, cache_weight,
        norm_gain[None, :], keep_rows[None, :], kept_count[None, :],
    )
    kept_cache = rotate_head(raw.astype(F32), positions).astype(BF)
    return (kept_hidden, kept_cache)


def solution(mesh):
    in_specs = (
        P("ctx", "tp"),
        P("ctx", "tp"),
        P("ctx", None),
        P("tp", "ctx"),
        P(),
        P(None, "tp"),
        P("ctx"),
        P("ctx"),
        P("ctx"),
    )
    out_specs = (P("ctx", "tp"), P("ctx", "tp"))
    fits = mesh.shape["ctx"] == 4 and mesh.shape["tp"] == 8
    body = fused_shards if fits else shards
    return jax.shard_map(body, mesh=mesh, in_specs=in_specs, out_specs=out_specs, check_vma=False)
```

```python
import math

import jax
import numpy as np
import jax.numpy as jnp
from jax import lax
from jax.experimental import pallas as pl
from jax.experimental.pallas import tpu as pltpu
from jax.sharding import PartitionSpec as P

D = 8192
HQ = 64
KVH = 8
HD = 128


THETA = 1000000.0
EPS = 1e-06


def rotate_pairs(cache_rows, position_ids, first_col, head_dim):
    pair_count = cache_rows.shape[1] // 2
    columns = first_col + 2 * jnp.arange(pair_count, dtype=jnp.int32)
    within = columns % (2 * head_dim)
    is_key = within < head_dim
    exponent = jnp.where(is_key, within, 0).astype(jnp.float32) / head_dim
    frequency = jnp.power(jnp.float32(THETA), -exponent)
    angles = position_ids.astype(jnp.float32)[:, None] * frequency[None, :]
    paired = cache_rows.reshape(cache_rows.shape[0], pair_count, 2)
    first_half = paired[..., 0]
    second = paired[..., 1]
    cosine = jnp.cos(angles)
    sine_rows = jnp.sin(angles)
    turned_first = first_half * cosine - second * sine_rows
    turned_second = second * cosine + first_half * sine_rows
    turned = jnp.stack(
        [jnp.where(is_key, turned_first, first_half), jnp.where(is_key, turned_second, second)], -1
    )
    return turned.reshape(cache_rows.shape)


def shards(
    residual,
    queries,
    keys_values,
    out_weight,
    norm_gain,
    cache_weight,
    positions,
    keep_rows,
    kept_count,
):
    row_count = residual.shape[0]
    ctx_index = lax.axis_index("ctx")
    tp_index = lax.axis_index("tp")
    head_count = queries.shape[1] // HD
    kv_head = tp_index * head_count // (HQ // KVH)
    head_block = lax.dynamic_slice_in_dim(keys_values, kv_head * 2 * HD, 2 * HD, 1)
    key_rows = head_block[:, :HD]
    value_rows = head_block[:, HD:]
    query_rows = queries.reshape(row_count, head_count, HD)
    own_index = ctx_index * row_count + jnp.arange(row_count, dtype=jnp.int32)
    score_scale = 1.0 / math.sqrt(HD)
    running_max = jnp.full((row_count, head_count), -1e30, jnp.float32)
    key_block = lax.all_gather(key_rows, "ctx", axis=0, tiled=True)
    value_block = lax.all_gather(value_rows, "ctx", axis=0, tiled=True)
    block_rows = key_block.shape[0]
    scores = (
        jnp.einsum("rgd,kd->rgk", query_rows, key_block, preferred_element_type=jnp.float32)
        * score_scale
    )
    visible = jnp.arange(block_rows, dtype=jnp.int32)[None, :] <= own_index[:, None]
    visible = visible[:, None, :]
    scores = jnp.where(visible, scores, -1e30)
    new_max = jnp.maximum(running_max, jnp.max(scores, axis=-1))
    weights = jnp.where(visible, jnp.exp(scores - new_max[..., None]), 0.0)
    new_sum = jnp.sum(weights, axis=-1)
    update = jnp.einsum(
        "rgk,kd->rgd", weights.astype(jnp.bfloat16), value_block, preferred_element_type=jnp.float32
    )
    attended = (
        (update / new_sum[..., None]).reshape(row_count, head_count * HD).astype(jnp.bfloat16)
    )
    own_count = kept_count[0]
    valid_rows = jnp.arange(row_count, dtype=jnp.int32) < own_count
    partials = jnp.dot(
        attended,
        lax.all_gather(out_weight, "ctx", axis=1, tiled=True),
        preferred_element_type=jnp.float32,
    )
    group_sums = lax.psum_scatter(
        partials.astype(jnp.bfloat16), "tp", scatter_dimension=1, tiled=True
    ).astype(jnp.float32)
    hidden = (residual.astype(jnp.float32) + group_sums).astype(jnp.bfloat16)
    feat_width = hidden.shape[1]
    wide_hidden = hidden.astype(jnp.float32)
    square_total = lax.psum(jnp.sum(wide_hidden * wide_hidden, axis=-1), "tp")
    inverse = lax.rsqrt(square_total / D + EPS)
    gain_part = lax.dynamic_slice_in_dim(norm_gain, tp_index * feat_width, feat_width)
    normed = (wide_hidden * inverse[:, None] * gain_part[None, :]).astype(jnp.bfloat16)
    gathered = lax.all_gather(normed, "tp", axis=1, tiled=True)
    cache_rows = jnp.dot(gathered, cache_weight, preferred_element_type=jnp.float32)
    cache_rot = rotate_pairs(cache_rows, positions, tp_index * cache_rows.shape[1], HD).astype(
        jnp.bfloat16
    )
    kept_flags = jnp.zeros((row_count,), jnp.int32).at[keep_rows].set(valid_rows.astype(jnp.int32))
    kept_mask = kept_flags[:, None] > 0
    kept_hidden = jnp.where(kept_mask, hidden, jnp.zeros_like(hidden))
    kept_cache = jnp.where(kept_mask, cache_rot, jnp.zeros_like(cache_rot))
    return (kept_hidden, kept_cache)


KEPT = 160
Z = 4
MESH = pl.DeviceIdType.MESH
BF = jnp.bfloat16
F32 = jnp.float32


def fused_kernel(
    q_hbm, r_hbm, kv_hbm, w_hbm, cw_hbm, gain_hbm, keep_hbm, count_ref, pos_ref, freq_ref,
    hid_out, cache_out,
    gain_ref, keep_ref, q_ref, r_ref, kvbuf, w_ref, cw_ref, qown, qrecv, rown, rrecv, resbuf, attb, ownp, ysend, yrecv,
    zsum, zrecv, xrecv, hbuf, ymsg, ymsg_in, cmsg, crecv, cbuf, hpair, cos_ref, sin_ref,
    loc_sem, kv_s, kv_r, q_s, q_r, res_s, res_r, att_s, att_r, y_s, y_r, z_s, z_r, x_r,
    ag_s, ag_r, fw_s, ay_s, ay_r, cw_s, cw_r, c_s, c_r, row_s, row_r, fin_s, fin_r,
):
    c = lax.axis_index("ctx")
    t = lax.axis_index("tp")
    p, k = c // 2, c % 2
    z, y = t // 2, t % 2
    rows = q_ref.shape[0]
    near = z + 1 - 2 * (z % 2)
    cross = Z - 1 - z
    is_inner = (z + 1) // 2 == 1

    def ctx_peer(i):
        return ((p + i // 2) % 2) * 2 + (k + i % 2) % 2

    sib = ctx_peer(1)
    ydev = (c, 2 * z + 1 - y)
    is_root = c == z
    pending = []

    def remote(src, dst, ss, rs, dev):
        return pltpu.make_async_remote_copy(
            src_ref=src, dst_ref=dst, send_sem=ss, recv_sem=rs, device_id=dev, device_id_type=MESH
        )

    def send(src, dst, ss, rs, dev):
        copy = remote(src, dst, ss, rs, dev)
        copy.start()
        pending.append(copy)
        return copy

    feat = cw_ref.shape[1]
    own_kv = kvbuf.at[pl.ds(pl.multiple_of(c * rows, rows), rows)]
    kv_copy = pltpu.make_async_copy(
        kv_hbm.at[:, pl.ds(pl.multiple_of(t * 2 * HD, 2 * HD), 2 * HD)], own_kv, loc_sem.at[2]
    )
    kv_copy.start()
    keep_load = pltpu.make_async_copy(keep_hbm, keep_ref, loc_sem.at[5])
    keep_load.start()
    q_load = pltpu.make_async_copy(q_hbm, q_ref, loc_sem.at[3])
    q_load.start()
    r_load = pltpu.make_async_copy(r_hbm, r_ref, loc_sem.at[4])
    r_load.start()
    w_copy = pltpu.make_async_copy(w_hbm, w_ref, loc_sem.at[0])
    w_copy.start()
    first_feat = pl.multiple_of((2 * c + y) * feat, feat)
    cw_copy = pltpu.make_async_copy(cw_hbm.at[pl.ds(first_feat, feat)], cw_ref.at[0], loc_sem.at[1])
    cw_copy.start()

    gain_load = pltpu.make_async_copy(gain_hbm, gain_ref, loc_sem.at[6])
    gain_load.start()

    barrier = pltpu.get_barrier_semaphore()
    partners = [(ctx_peer(i), t) for i in (1, 2, 3)]
    partners += [(c, zz * 2 + y) for zz in (near, cross)] + [ydev]
    for dev in partners:
        pl.semaphore_signal(barrier, inc=1, device_id=dev, device_id_type=MESH)
    pl.semaphore_wait(barrier, len(partners))

    count = count_ref[...]
    keep_load.wait()
    base = jnp.where(k == 0, 0, 2 * KEPT - count)
    chosen = keep_ref[...] == lax.broadcasted_iota(jnp.int32, (rows, rows), 0)
    rank = lax.broadcasted_iota(jnp.int32, (rows, KEPT), 0)
    slot_at = lax.broadcasted_iota(jnp.int32, (rows, KEPT), 1)
    chosen = jnp.where(chosen, 1.0, 0.0).astype(BF)

    def place_of(kk):
        hit = (rank + base == slot_at + kk * KEPT) & (rank < count)
        return jnp.dot(
            chosen, jnp.where(hit, 1.0, 0.0).astype(BF), preferred_element_type=F32
        ).astype(BF)

    place_sib = place_of(1 - k)
    place_own = place_of(k)
    row_id = lax.broadcasted_iota(jnp.int32, (rows, HD), 0).astype(F32)
    lane = lax.broadcasted_iota(jnp.int32, (rows, HD), 1)
    tags = jnp.where(lane == 0, row_id, jnp.where(lane == 1, 1.0, 0.0)).astype(BF)
    width = q_ref.shape[1]

    def pick(sel, what):
        return lax.dot_general(
            sel, what, (((0,), (0,)), ((), ())), preferred_element_type=F32
        ).astype(BF)

    kv_copy.wait()
    kv_far = send(own_kv, own_kv, kv_s.at[0], kv_r.at[0], (ctx_peer(2), t))
    kv_sib = send(own_kv, own_kv, kv_s.at[1], kv_r.at[1], (sib, t))
    cw_send = send(
        cw_hbm.at[pl.ds(pl.multiple_of((2 * c + 1 - y) * feat, feat), feat)],
        cw_ref.at[1], cw_s, cw_r, ydev,
    )
    q_load.wait()
    qown[0, :, :width] = pick(place_sib, q_ref[...])
    qown[0, :, width:] = pick(place_sib, tags)
    q_copy = send(qown.at[0], qrecv, q_s.at[0], q_r.at[0], (sib, t))
    r_load.wait()
    rown[0] = pick(place_sib, r_ref[...])
    r_copy = send(rown.at[0], rrecv, q_s.at[1], q_r.at[1], (sib, t))
    qown[1, :, :width] = pick(place_own, q_ref[...])
    qown[1, :, width:] = pick(place_own, tags)
    rown[1] = pick(place_own, r_ref[...])

    kv_far.wait_recv()
    far_kv = kvbuf.at[pl.ds(pl.multiple_of(ctx_peer(2) * rows, rows), rows)]
    kv_diag = send(far_kv, far_kv, kv_s.at[2], kv_r.at[2], (sib, t))
    q_copy.wait_recv()
    own_tag = qown[1, :, width:].astype(F32)
    sib_tag = qrecv[:, width:].astype(F32)
    first_own = (c * rows).astype(F32)
    first_sib = (sib * rows).astype(F32)
    limit = (
        own_tag[:, 0:1] + first_own * own_tag[:, 1:2] + sib_tag[:, 0:1] + first_sib * sib_tag[:, 1:2]
    )
    qown[1, :, :width] = qown[1, :, :width] + qrecv[:, :width]

    r_copy.wait_recv()
    rown[1] = rown[1] + rrecv[...]
    res_slot = ((p + z // 2) % 2) * 2 + (k + z) % 2
    res_copy = remote(
        rown.at[1], resbuf.at[res_slot], res_s, res_r.at[res_slot], (z, t)
    )

    @pl.when(is_root)
    def _():
        resbuf[0] = rown[1]

    @pl.when(jnp.logical_not(is_root))
    def _():
        res_copy.start()

    kv_sib.wait_recv()
    kv_diag.wait_recv()
    total = kvbuf.shape[0]
    col_id = lax.broadcasted_iota(jnp.int32, (KEPT, total), 1).astype(F32)
    group = 4
    seen = col_id <= limit
    seen = jnp.concatenate([seen] * group, axis=0)
    scale = math.log2(math.e) / math.sqrt(HD)
    keys = kvbuf[:, :HD]
    values = kvbuf[:, HD:]
    for first in range(0, width // HD, group):
        heads = [slice(h * HD, (h + 1) * HD) for h in range(first, first + group)]
        s = lax.dot_general(
            jnp.concatenate([qown[1, :, cols] for cols in heads], axis=0),
            keys,
            (((1,), (1,)), ((), ())),
            preferred_element_type=F32,
        )
        s = jnp.where(seen, s, -1e30)
        top = jnp.max(s, axis=1, keepdims=True)
        e = jnp.exp2((s - top) * scale)
        den = jnp.sum(e, axis=1, keepdims=True)
        mixed = jnp.dot(e.astype(BF), values, preferred_element_type=F32) / den
        for n, cols in enumerate(heads):
            attb[0, :, cols] = mixed[n * KEPT : (n + 1) * KEPT].astype(BF)

    att_cp = send(attb.at[0], attb.at[2], att_s.at[0], att_r.at[0], (ctx_peer(2), t))
    att_sib = send(attb.at[0], attb.at[1], att_s.at[1], att_r.at[1], (sib, t))
    half = Z * 256
    other = 2 * (1 - z // 2)
    mine = 2 - other
    is_outer = jnp.logical_not(is_inner)
    near_dev = (c, near * 2 + y)
    cross_dev = (c, cross * 2 + y)
    sequence = [(jj, other + jj) for jj in range(2)] + [(2 + jj, mine + jj) for jj in range(2)]

    def piece_of(who, j):
        return pl.ds(pl.multiple_of(who * half + j * 256, 256), 256)

    def y_copy(i, j):
        return remote(ysend.at[i, j], yrecv.at[i, j], y_s.at[i, j], y_r.at[i, j], ydev)

    def out_copy(i, j):
        return remote(zsum.at[i, j], zrecv.at[i, j], z_s.at[i, j], z_r.at[i, j], near_dev)

    def cross_copy(i, j):
        return remote(zsum.at[i, j], xrecv.at[i, j], z_s.at[i, j], x_r.at[i, j], cross_dev)
    w_copy.wait()
    fwd = {}
    ays, cs = {}, {}

    def stage_a(i):
        if i == 1:
            att_sib.wait_recv()
        if i == 2:
            att_cp.wait_recv()
            fwd[0] = send(attb.at[2], attb.at[3], att_s.at[2], att_r.at[2], (sib, t))
        if i == 3:
            fwd[0].wait_recv()
        for _, j in sequence:
            ysend[i, j] = jnp.dot(
                attb[i], w_ref[:, piece_of(1 - y, j)], preferred_element_type=F32
            ).astype(BF)
            copy = y_copy(i, j)
            copy.start()
            pending.append(copy)
        for _, j in sequence:
            ownp[i, j] = jnp.dot(
                attb[i], w_ref[:, piece_of(y, j)], preferred_element_type=F32
            )

    def stage_b(i):
        @pl.when(is_root)
        def _():
            if i > 0:
                remote(
                    rown.at[1], resbuf.at[i], res_s, res_r.at[i], (ctx_peer(i), t)
                ).wait_recv()
            for j in range(Z):
                ownp[i, j] = ownp[i, j] + resbuf[i, :, j * 256 : (j + 1) * 256].astype(F32)

        for _, j in sequence:
            y_copy(i, j).wait_recv()
            total = ownp[i, j] + yrecv[i, j].astype(F32)

            @pl.when(is_outer)
            def _():
                zsum[i, j] = total.astype(BF)
                out_copy(i, j).start()

            @pl.when(is_inner)
            def _():
                ownp[i, j] = total

    def stage_g(i):
        @pl.when(is_inner)
        def _():
            for n, j in sequence:
                out_copy(i, j).wait_recv()
                total = ownp[i, j] + zrecv[i, j].astype(F32)
                if n < 2:
                    zsum[i, j] = total.astype(BF)
                    cross_copy(i, j).start()
                else:
                    ownp[i, j] = total

    def piece_copy(i, j, dev, sem):
        piece = hbuf.at[i, j]
        return remote(piece, piece, sem.at[i, j], ag_r.at[i, j], dev)

    def stage_c(i):
        @pl.when(is_inner)
        def _():
            for n, j in sequence[2:]:
                cross_copy(i, j).wait_recv()
                hbuf[i, j] = (ownp[i, j] + xrecv[i, j].astype(F32)).astype(BF)
                piece_copy(i, j, cross_dev, ag_s).start()
                piece_copy(i, j, near_dev, fw_s).start()

    def stage_f(i):
        @pl.when(is_inner)
        def _():
            for n, j in sequence[:2]:
                piece_copy(i, j, cross_dev, ag_s).wait_recv()
                piece_copy(i, j, near_dev, fw_s).start()

    def row_copy(i):
        return remote(
            hbuf.at[i], hpair.at[(k + i % 2) % 2], row_s.at[i], row_r, (ctx_peer(i), t)
        )

    own_part = {}

    def packed(acc, squares):
        coarse = squares.astype(BF).astype(F32)
        at = lax.broadcasted_iota(jnp.int32, (KEPT, HD), 1)
        tail = jnp.where(at == 0, coarse, jnp.where(at == 1, squares - coarse, 0.0))
        return acc.astype(BF), tail.astype(BF)

    def unpacked(ref, i):
        tail = ref[i, :, 256:].astype(F32)
        return ref[i, :, :256].astype(F32), tail[:, 0:1] + tail[:, 1:2]

    def stage_d(i):
        @pl.when(is_outer)
        def _():
            for _, j in sequence[2:] + sequence[:2]:
                piece_copy(i, j, near_dev, fw_s).wait_recv()

        @pl.when(is_root)
        def _():
            if i == 0:
                hpair[k] = hbuf[i]
            else:
                row_copy(i).start()

        if i == 0:
            gain_load.wait()
            cw_copy.wait()
            cw_send.wait_recv()
        far = jnp.zeros((KEPT, 256), F32)
        acc = jnp.zeros((KEPT, 256), F32)
        squares = jnp.zeros((KEPT, 1), F32)
        for q in range(Z):
            wide = hbuf[i, q].astype(F32)
            squares = squares + jnp.sum(wide * wide, axis=1, keepdims=True)
            gain = gain_ref[:, pl.ds(pl.multiple_of(first_feat + q * 256, 256), 256)]
            scaled = (wide * gain).astype(BF)
            cut = slice(q * 256, (q + 1) * 256)
            far = far + jnp.dot(scaled, cw_ref[1, cut], preferred_element_type=F32)
            acc = acc + jnp.dot(scaled, cw_ref[0, cut], preferred_element_type=F32)
        ymsg[i, :, :256], ymsg[i, :, 256:] = packed(far, squares)
        ays[i] = send(ymsg.at[i], ymsg_in.at[i], ay_s.at[i], ay_r.at[i], ydev)
        own_part[i] = acc, squares

    def stage_e(i):
        ays[i].wait_recv()
        acc, squares = own_part[i]
        more, more_squares = unpacked(ymsg_in, i)
        acc = acc + more
        squares = squares + more_squares
        if i == 0:
            return acc, squares
        cmsg[i - 1, :, :256], cmsg[i - 1, :, 256:] = packed(acc, squares)
        cs[i] = send(
            cmsg.at[i - 1], crecv.at[i - 1], c_s.at[i - 1], c_r.at[i - 1], (ctx_peer(i), t)
        )
        return None

    stage_a(0)
    stage_a(1)
    diagonal = lax.broadcasted_iota(jnp.int32, (rows, rows), 0) == lax.broadcasted_iota(
        jnp.int32, (rows, rows), 1
    )
    at_row = jnp.sum(
        jnp.where(diagonal, pos_ref[...].astype(F32), 0.0), axis=1, keepdims=True
    )
    angles = at_row * freq_ref[...]
    cos_ref[...] = jnp.cos(angles)
    sin_ref[...] = jnp.sin(angles)
    stage_b(0)
    stage_a(2)
    stage_g(0)
    stage_c(0)
    stage_b(1)
    stage_a(3)
    stage_f(0)
    stage_g(1)
    stage_d(0)
    stage_c(1)
    stage_b(2)
    stage_f(1)
    stage_g(2)
    stage_d(1)
    stage_c(2)
    stage_b(3)
    stage_f(2)
    stage_g(3)
    stage_e(1)
    stage_d(2)
    stage_c(3)
    stage_f(3)
    stage_e(2)
    stage_d(3)

    stage_e(3)
    acc, squares = stage_e(0)

    @pl.when(jnp.logical_not(is_root))
    def _():
        row_copy(1).wait_recv()

    pair_copy = send(hpair.at[k], hpair.at[k], fin_s.at[0], fin_r.at[0], (sib, t))
    for i in (1, 2, 3):
        cs[i].wait_recv()
        more, more_squares = unpacked(crecv, i - 1)
        acc = acc + more
        squares = squares + more_squares
    cbuf[k] = (acc * lax.rsqrt(squares / D + EPS)).astype(BF)
    last = send(cbuf.at[k], cbuf.at[k], fin_s.at[1], fin_r.at[1], (sib, t))
    place = [place_of(kk) for kk in range(2)]
    pair_copy.wait_recv()
    for j in range(Z):
        hid_out[:, j * 256 : (j + 1) * 256] = (
            jnp.dot(place[0], hpair[0, j], preferred_element_type=F32)
            + jnp.dot(place[1], hpair[1, j], preferred_element_type=F32)
        ).astype(BF)
    last.wait_recv()
    raw = jnp.dot(place[0], cbuf[0], preferred_element_type=F32) + jnp.dot(
        place[1], cbuf[1], preferred_element_type=F32
    )
    source = lax.broadcasted_iota(jnp.int32, (HD, HD), 0)
    target = lax.broadcasted_iota(jnp.int32, (HD, HD), 1)
    swap = jnp.where(
        source == target + 1, jnp.where(target % 2 == 0, -1.0, 0.0),
        jnp.where(source == target - 1, jnp.where(target % 2 == 1, 1.0, 0.0), 0.0),
    ).astype(BF)
    key = raw[:, :HD]
    partner = jnp.dot(key.astype(BF), swap, preferred_element_type=F32)
    cache_out[:, :HD] = (key * cos_ref[...] + partner * sin_ref[...]).astype(BF)
    cache_out[:, HD:] = raw[:, HD:].astype(BF)

    for copy in pending:
        copy.wait_send()

    @pl.when(jnp.logical_not(is_root))
    def _():
        res_copy.wait_send()

    @pl.when(is_root)
    def _():
        for i in (1, 2, 3):
            row_copy(i).wait_send()

    @pl.when(is_inner)
    def _():
        for i in range(4):
            for n, j in sequence:
                piece_copy(i, j, near_dev, fw_s).wait_send()
                if n < 2:
                    cross_copy(i, j).wait_send()
                else:
                    piece_copy(i, j, cross_dev, ag_s).wait_send()

    @pl.when(is_outer)
    def _():
        for i in range(4):
            for _, j in sequence:
                out_copy(i, j).wait_send()


def fused_shards(
    residual, queries, keys_values, out_weight, norm_gain, cache_weight, positions, keep_rows, kept_count
):
    rows, width = queries.shape
    pair_first = np.arange(HD) // 2 * 2
    frequency = jnp.asarray(np.power(THETA, -pair_first / HD).astype(np.float32)[None, :])
    feat = out_weight.shape[1]
    n_ctx = D // feat
    dma = pltpu.SemaphoreType.DMA
    vmem = pl.BlockSpec(memory_space=pltpu.VMEM)
    hbm = pl.BlockSpec(memory_space=pl.ANY)
    return pl.pallas_call(
        fused_kernel,
        out_shape=(
            jax.ShapeDtypeStruct((rows, width), BF),
            jax.ShapeDtypeStruct((rows, 2 * HD), BF),
        ),
        in_specs=[hbm] * 7 + [vmem] * 3,
        out_specs=(vmem, vmem),
        scratch_shapes=[
            pltpu.VMEM((1, D), F32),
            pltpu.VMEM((1, rows), jnp.int32),
            pltpu.VMEM((rows, width), BF),
            pltpu.VMEM((rows, width), BF),
            pltpu.VMEM((n_ctx * rows, 2 * HD), BF),
            pltpu.VMEM(out_weight.shape, BF),
            pltpu.VMEM((2, feat // 2, 2 * HD), BF),
            pltpu.VMEM((2, KEPT, width + HD), BF),
            pltpu.VMEM((KEPT, width + HD), BF),
            pltpu.VMEM((2, KEPT, width), BF),
            pltpu.VMEM((KEPT, width), BF),
            pltpu.VMEM((4, KEPT, width), BF),
            pltpu.VMEM((4, KEPT, width), BF),
            pltpu.VMEM((4, Z, KEPT, 256), F32),
            pltpu.VMEM((4, Z, KEPT, 256), BF),
            pltpu.VMEM((4, Z, KEPT, 256), BF),
            pltpu.VMEM((4, Z, KEPT, 256), BF),
            pltpu.VMEM((4, Z, KEPT, 256), BF),
            pltpu.VMEM((4, Z, KEPT, 256), BF),
            pltpu.VMEM((4, Z, KEPT, 256), BF),
            pltpu.VMEM((4, KEPT, 256 + HD), BF),
            pltpu.VMEM((4, KEPT, 256 + HD), BF),
            pltpu.VMEM((3, KEPT, 256 + HD), BF),
            pltpu.VMEM((3, KEPT, 256 + HD), BF),
            pltpu.VMEM((2, KEPT, 256), BF),
            pltpu.VMEM((2, Z, KEPT, 256), BF),
            pltpu.VMEM((rows, HD), F32),
            pltpu.VMEM((rows, HD), F32),
            dma((7,)), dma((3,)), dma((3,)), dma((2,)), dma((2,)), dma, dma((4,)),
            dma((3,)), dma((3,)), dma((4, 4)), dma((4, 4)), dma((4, 4)), dma((4, 4)), dma((4, 4)),
            dma((4, 4)), dma((4, 4)), dma((4, 4)), dma((4,)), dma((4,)), dma, dma, dma((3,)), dma((3,)),
            dma((4,)), dma, dma((2,)), dma((2,)),
        ],
        compiler_params=pltpu.CompilerParams(
            collective_id=0, has_side_effects=True, vmem_limit_bytes=60 * 1024 * 1024
        ),
        cost_estimate=pl.CostEstimate(flops=6_000_000_000, bytes_accessed=8_000_000, transcendentals=1_400_000),
    )(
        queries, residual, keys_values, out_weight, cache_weight,
        norm_gain[None, :], keep_rows[None, :], kept_count[None, :],
        positions[None, :], frequency,
    )


def solution(mesh):
    in_specs = (
        P("ctx", "tp"),
        P("ctx", "tp"),
        P("ctx", None),
        P("tp", "ctx"),
        P(),
        P(None, "tp"),
        P("ctx"),
        P("ctx"),
        P("ctx"),
    )
    out_specs = (P("ctx", "tp"), P("ctx", "tp"))
    fits = mesh.shape["ctx"] == 4 and mesh.shape["tp"] == 8
    body = fused_shards if fits else shards
    return jax.shard_map(body, mesh=mesh, in_specs=in_specs, out_specs=out_specs, check_vma=False)
```

```python
import math

import jax
import numpy as np
import jax.numpy as jnp
from jax import lax
from jax.experimental import pallas as pl
from jax.experimental.pallas import tpu as pltpu
from jax.sharding import PartitionSpec as P

D = 8192
HQ = 64
KVH = 8
HD = 128


THETA = 1000000.0
EPS = 1e-06


def rotate_pairs(cache_rows, position_ids, first_col, head_dim):
    pair_count = cache_rows.shape[1] // 2
    columns = first_col + 2 * jnp.arange(pair_count, dtype=jnp.int32)
    within = columns % (2 * head_dim)
    is_key = within < head_dim
    exponent = jnp.where(is_key, within, 0).astype(jnp.float32) / head_dim
    frequency = jnp.power(jnp.float32(THETA), -exponent)
    angles = position_ids.astype(jnp.float32)[:, None] * frequency[None, :]
    paired = cache_rows.reshape(cache_rows.shape[0], pair_count, 2)
    first_half = paired[..., 0]
    second = paired[..., 1]
    cosine = jnp.cos(angles)
    sine_rows = jnp.sin(angles)
    turned_first = first_half * cosine - second * sine_rows
    turned_second = second * cosine + first_half * sine_rows
    turned = jnp.stack(
        [jnp.where(is_key, turned_first, first_half), jnp.where(is_key, turned_second, second)], -1
    )
    return turned.reshape(cache_rows.shape)


def shards(
    residual,
    queries,
    keys_values,
    out_weight,
    norm_gain,
    cache_weight,
    positions,
    keep_rows,
    kept_count,
):
    row_count = residual.shape[0]
    ctx_index = lax.axis_index("ctx")
    tp_index = lax.axis_index("tp")
    head_count = queries.shape[1] // HD
    kv_head = tp_index * head_count // (HQ // KVH)
    head_block = lax.dynamic_slice_in_dim(keys_values, kv_head * 2 * HD, 2 * HD, 1)
    key_rows = head_block[:, :HD]
    value_rows = head_block[:, HD:]
    query_rows = queries.reshape(row_count, head_count, HD)
    own_index = ctx_index * row_count + jnp.arange(row_count, dtype=jnp.int32)
    score_scale = 1.0 / math.sqrt(HD)
    running_max = jnp.full((row_count, head_count), -1e30, jnp.float32)
    key_block = lax.all_gather(key_rows, "ctx", axis=0, tiled=True)
    value_block = lax.all_gather(value_rows, "ctx", axis=0, tiled=True)
    block_rows = key_block.shape[0]
    scores = (
        jnp.einsum("rgd,kd->rgk", query_rows, key_block, preferred_element_type=jnp.float32)
        * score_scale
    )
    visible = jnp.arange(block_rows, dtype=jnp.int32)[None, :] <= own_index[:, None]
    visible = visible[:, None, :]
    scores = jnp.where(visible, scores, -1e30)
    new_max = jnp.maximum(running_max, jnp.max(scores, axis=-1))
    weights = jnp.where(visible, jnp.exp(scores - new_max[..., None]), 0.0)
    new_sum = jnp.sum(weights, axis=-1)
    update = jnp.einsum(
        "rgk,kd->rgd", weights.astype(jnp.bfloat16), value_block, preferred_element_type=jnp.float32
    )
    attended = (
        (update / new_sum[..., None]).reshape(row_count, head_count * HD).astype(jnp.bfloat16)
    )
    own_count = kept_count[0]
    valid_rows = jnp.arange(row_count, dtype=jnp.int32) < own_count
    partials = jnp.dot(
        attended,
        lax.all_gather(out_weight, "ctx", axis=1, tiled=True),
        preferred_element_type=jnp.float32,
    )
    group_sums = lax.psum_scatter(
        partials.astype(jnp.bfloat16), "tp", scatter_dimension=1, tiled=True
    ).astype(jnp.float32)
    hidden = (residual.astype(jnp.float32) + group_sums).astype(jnp.bfloat16)
    feat_width = hidden.shape[1]
    wide_hidden = hidden.astype(jnp.float32)
    square_total = lax.psum(jnp.sum(wide_hidden * wide_hidden, axis=-1), "tp")
    inverse = lax.rsqrt(square_total / D + EPS)
    gain_part = lax.dynamic_slice_in_dim(norm_gain, tp_index * feat_width, feat_width)
    normed = (wide_hidden * inverse[:, None] * gain_part[None, :]).astype(jnp.bfloat16)
    gathered = lax.all_gather(normed, "tp", axis=1, tiled=True)
    cache_rows = jnp.dot(gathered, cache_weight, preferred_element_type=jnp.float32)
    cache_rot = rotate_pairs(cache_rows, positions, tp_index * cache_rows.shape[1], HD).astype(
        jnp.bfloat16
    )
    kept_flags = jnp.zeros((row_count,), jnp.int32).at[keep_rows].set(valid_rows.astype(jnp.int32))
    kept_mask = kept_flags[:, None] > 0
    kept_hidden = jnp.where(kept_mask, hidden, jnp.zeros_like(hidden))
    kept_cache = jnp.where(kept_mask, cache_rot, jnp.zeros_like(cache_rot))
    return (kept_hidden, kept_cache)


KEPT = 160
Z = 4
MESH = pl.DeviceIdType.MESH
BF = jnp.bfloat16
F32 = jnp.float32


def fused_kernel(
    q_hbm, r_hbm, kv_hbm, w_hbm, cw_hbm, gain_hbm, keep_hbm, count_ref, pos_ref, freq_ref,
    hid_out, cache_out,
    gain_ref, keep_ref, q_ref, r_ref, kvbuf, w_ref, cw_ref, qown, qrecv, rown, rrecv, resbuf, attb, ownp, ysend, yrecv,
    zsum, zrecv, xrecv, hbuf, ymsg, ymsg_in, cmsg, crecv, cbuf, hpair, cos_ref, sin_ref,
    loc_sem, kv_s, kv_r, q_s, q_r, res_s, res_r, att_s, att_r, y_s, y_r, z_s, z_r, x_r,
    ag_s, ag_r, fw_s, ay_s, ay_r, cw_s, cw_r, c_s, c_r, row_s, row_r, fin_s, fin_r,
):
    c = lax.axis_index("ctx")
    t = lax.axis_index("tp")
    p, k = c // 2, c % 2
    z, y = t // 2, t % 2
    rows = q_ref.shape[0]
    near = z + 1 - 2 * (z % 2)
    cross = Z - 1 - z
    is_inner = (z + 1) // 2 == 1

    def ctx_peer(i):
        return ((p + i // 2) % 2) * 2 + (k + i % 2) % 2

    sib = ctx_peer(1)
    ydev = (c, 2 * z + 1 - y)
    is_root = c == z
    pending = []

    def remote(src, dst, ss, rs, dev):
        return pltpu.make_async_remote_copy(
            src_ref=src, dst_ref=dst, send_sem=ss, recv_sem=rs, device_id=dev, device_id_type=MESH
        )

    def send(src, dst, ss, rs, dev):
        copy = remote(src, dst, ss, rs, dev)
        copy.start()
        pending.append(copy)
        return copy

    feat = cw_ref.shape[1]
    own_kv = kvbuf.at[pl.ds(pl.multiple_of(c * rows, rows), rows)]
    kv_copy = pltpu.make_async_copy(
        kv_hbm.at[:, pl.ds(pl.multiple_of(t * 2 * HD, 2 * HD), 2 * HD)], own_kv, loc_sem.at[2]
    )
    kv_copy.start()
    keep_load = pltpu.make_async_copy(keep_hbm, keep_ref, loc_sem.at[5])
    keep_load.start()
    q_load = pltpu.make_async_copy(q_hbm, q_ref, loc_sem.at[3])
    q_load.start()
    r_load = pltpu.make_async_copy(r_hbm, r_ref, loc_sem.at[4])
    r_load.start()
    w_copy = pltpu.make_async_copy(w_hbm, w_ref, loc_sem.at[0])
    w_copy.start()
    first_feat = pl.multiple_of((2 * c + y) * feat, feat)
    cw_copy = pltpu.make_async_copy(cw_hbm.at[pl.ds(first_feat, feat)], cw_ref.at[0], loc_sem.at[1])
    cw_copy.start()

    gain_load = pltpu.make_async_copy(gain_hbm, gain_ref, loc_sem.at[6])
    gain_load.start()

    barrier = pltpu.get_barrier_semaphore()
    partners = [(ctx_peer(i), t) for i in (1, 2, 3)]
    partners += [(c, zz * 2 + y) for zz in (near, cross)] + [ydev]
    for dev in partners:
        pl.semaphore_signal(barrier, inc=1, device_id=dev, device_id_type=MESH)
    pl.semaphore_wait(barrier, len(partners))

    count = count_ref[...]
    keep_load.wait()
    base = jnp.where(k == 0, 0, 2 * KEPT - count)
    chosen = keep_ref[...] == lax.broadcasted_iota(jnp.int32, (rows, rows), 0)
    rank = lax.broadcasted_iota(jnp.int32, (rows, KEPT), 0)
    slot_at = lax.broadcasted_iota(jnp.int32, (rows, KEPT), 1)
    chosen = jnp.where(chosen, 1.0, 0.0).astype(BF)

    def place_of(kk):
        hit = (rank + base == slot_at + kk * KEPT) & (rank < count)
        return jnp.dot(
            chosen, jnp.where(hit, 1.0, 0.0).astype(BF), preferred_element_type=F32
        ).astype(BF)

    place_sib = place_of(1 - k)
    place_own = place_of(k)
    row_id = lax.broadcasted_iota(jnp.int32, (rows, HD), 0).astype(F32)
    lane = lax.broadcasted_iota(jnp.int32, (rows, HD), 1)
    tags = jnp.where(lane == 0, row_id, jnp.where(lane == 1, 1.0, 0.0)).astype(BF)
    width = q_ref.shape[1]

    def pick(sel, what):
        return lax.dot_general(
            sel, what, (((0,), (0,)), ((), ())), preferred_element_type=F32
        ).astype(BF)

    kv_copy.wait()
    kv_far = send(own_kv, own_kv, kv_s.at[0], kv_r.at[0], (ctx_peer(2), t))
    kv_sib = send(own_kv, own_kv, kv_s.at[1], kv_r.at[1], (sib, t))
    cw_send = send(
        cw_hbm.at[pl.ds(pl.multiple_of((2 * c + 1 - y) * feat, feat), feat)],
        cw_ref.at[1], cw_s, cw_r, ydev,
    )
    q_load.wait()
    qown[0, :, :width] = pick(place_sib, q_ref[...])
    qown[0, :, width:] = pick(place_sib, tags)
    q_copy = send(qown.at[0], qrecv, q_s.at[0], q_r.at[0], (sib, t))
    r_load.wait()
    rown[0] = pick(place_sib, r_ref[...])
    r_copy = send(rown.at[0], rrecv, q_s.at[1], q_r.at[1], (sib, t))
    qown[1, :, :width] = pick(place_own, q_ref[...])
    qown[1, :, width:] = pick(place_own, tags)
    rown[1] = pick(place_own, r_ref[...])

    kv_far.wait_recv()
    far_kv = kvbuf.at[pl.ds(pl.multiple_of(ctx_peer(2) * rows, rows), rows)]
    kv_diag = send(far_kv, far_kv, kv_s.at[2], kv_r.at[2], (sib, t))
    q_copy.wait_recv()
    own_tag = qown[1, :, width:].astype(F32)
    sib_tag = qrecv[:, width:].astype(F32)
    first_own = (c * rows).astype(F32)
    first_sib = (sib * rows).astype(F32)
    limit = (
        own_tag[:, 0:1] + first_own * own_tag[:, 1:2] + sib_tag[:, 0:1] + first_sib * sib_tag[:, 1:2]
    )
    qown[1, :, :width] = qown[1, :, :width] + qrecv[:, :width]

    r_copy.wait_recv()
    rown[1] = rown[1] + rrecv[...]
    res_slot = ((p + z // 2) % 2) * 2 + (k + z) % 2
    res_copy = remote(
        rown.at[1], resbuf.at[res_slot], res_s, res_r.at[res_slot], (z, t)
    )

    @pl.when(is_root)
    def _():
        resbuf[0] = rown[1]

    @pl.when(jnp.logical_not(is_root))
    def _():
        res_copy.start()

    kv_sib.wait_recv()
    kv_diag.wait_recv()
    total = kvbuf.shape[0]
    col_id = lax.broadcasted_iota(jnp.int32, (KEPT, total), 1).astype(F32)
    group = 4
    seen = col_id <= limit
    seen = jnp.concatenate([seen] * group, axis=0)
    scale = math.log2(math.e) / math.sqrt(HD)
    keys = kvbuf[:, :HD]
    values = kvbuf[:, HD:]
    for first in range(0, width // HD, group):
        heads = [slice(h * HD, (h + 1) * HD) for h in range(first, first + group)]
        s = lax.dot_general(
            jnp.concatenate([qown[1, :, cols] for cols in heads], axis=0),
            keys,
            (((1,), (1,)), ((), ())),
            preferred_element_type=F32,
        )
        s = jnp.where(seen, s, -1e30)
        top = jnp.max(s, axis=1, keepdims=True)
        e = jnp.exp2((s - top) * scale)
        den = jnp.sum(e, axis=1, keepdims=True)
        mixed = jnp.dot(e.astype(BF), values, preferred_element_type=F32) / den
        for n, cols in enumerate(heads):
            attb[0, :, cols] = mixed[n * KEPT : (n + 1) * KEPT].astype(BF)

    att_cp = send(attb.at[0], attb.at[2], att_s.at[0], att_r.at[0], (ctx_peer(2), t))
    att_sib = send(attb.at[0], attb.at[1], att_s.at[1], att_r.at[1], (sib, t))
    half = Z * 256
    other = 2 * (1 - z // 2)
    mine = 2 - other
    is_outer = jnp.logical_not(is_inner)
    near_dev = (c, near * 2 + y)
    cross_dev = (c, cross * 2 + y)
    sequence = [(jj, other + jj) for jj in range(2)] + [(2 + jj, mine + jj) for jj in range(2)]

    def piece_of(who, j):
        return pl.ds(pl.multiple_of(who * half + j * 256, 256), 256)

    def y_copy(i, j):
        return remote(ysend.at[i, j], yrecv.at[i, j], y_s.at[i, j], y_r.at[i, j], ydev)

    def out_copy(i, j):
        return remote(zsum.at[i, j], zrecv.at[i, j], z_s.at[i, j], z_r.at[i, j], near_dev)

    def cross_copy(i, j):
        return remote(zsum.at[i, j], xrecv.at[i, j], z_s.at[i, j], x_r.at[i, j], cross_dev)
    w_copy.wait()
    fwd = {}
    ays, cs = {}, {}

    def stage_a(i):
        if i == 1:
            att_sib.wait_recv()
        if i == 2:
            att_cp.wait_recv()
            fwd[0] = send(attb.at[2], attb.at[3], att_s.at[2], att_r.at[2], (sib, t))
        if i == 3:
            fwd[0].wait_recv()
        for _, j in sequence:
            ysend[i, j] = jnp.dot(
                attb[i], w_ref[:, piece_of(1 - y, j)], preferred_element_type=F32
            ).astype(BF)
            copy = y_copy(i, j)
            copy.start()
            pending.append(copy)
        for _, j in sequence:
            ownp[i, j] = jnp.dot(
                attb[i], w_ref[:, piece_of(y, j)], preferred_element_type=F32
            )

    def stage_b(i):
        @pl.when(is_root)
        def _():
            if i > 0:
                remote(
                    rown.at[1], resbuf.at[i], res_s, res_r.at[i], (ctx_peer(i), t)
                ).wait_recv()
            for j in range(Z):
                ownp[i, j] = ownp[i, j] + resbuf[i, :, j * 256 : (j + 1) * 256].astype(F32)

        for _, j in sequence:
            y_copy(i, j).wait_recv()
            total = ownp[i, j] + yrecv[i, j].astype(F32)

            @pl.when(is_outer)
            def _():
                zsum[i, j] = total.astype(BF)
                out_copy(i, j).start()

            @pl.when(is_inner)
            def _():
                ownp[i, j] = total

    def stage_g(i):
        @pl.when(is_inner)
        def _():
            for n, j in sequence:
                out_copy(i, j).wait_recv()
                total = ownp[i, j] + zrecv[i, j].astype(F32)
                if n < 2:
                    zsum[i, j] = total.astype(BF)
                    cross_copy(i, j).start()
                else:
                    ownp[i, j] = total

    def piece_copy(i, j, dev, sem):
        piece = hbuf.at[i, j]
        return remote(piece, piece, sem.at[i, j], ag_r.at[i, j], dev)

    def stage_c(i):
        @pl.when(is_inner)
        def _():
            for n, j in sequence[2:]:
                cross_copy(i, j).wait_recv()
                hbuf[i, j] = (ownp[i, j] + xrecv[i, j].astype(F32)).astype(BF)
                piece_copy(i, j, cross_dev, ag_s).start()
                piece_copy(i, j, near_dev, fw_s).start()

    def stage_f(i):
        @pl.when(is_inner)
        def _():
            for n, j in sequence[:2]:
                piece_copy(i, j, cross_dev, ag_s).wait_recv()
                piece_copy(i, j, near_dev, fw_s).start()

    def row_copy(i):
        return remote(
            hbuf.at[i], hpair.at[(k + i % 2) % 2], row_s.at[i], row_r, (ctx_peer(i), t)
        )

    own_part = {}

    def packed(acc, squares):
        coarse = squares.astype(BF).astype(F32)
        at = lax.broadcasted_iota(jnp.int32, (KEPT, HD), 1)
        tail = jnp.where(at == 0, coarse, jnp.where(at == 1, squares - coarse, 0.0))
        return acc.astype(BF), tail.astype(BF)

    def unpacked(ref, i):
        tail = ref[i, :, 256:].astype(F32)
        return ref[i, :, :256].astype(F32), tail[:, 0:1] + tail[:, 1:2]

    def stage_d(i):
        @pl.when(is_outer)
        def _():
            for _, j in sequence[2:] + sequence[:2]:
                piece_copy(i, j, near_dev, fw_s).wait_recv()

        @pl.when(is_root)
        def _():
            if i == 0:
                hpair[k] = hbuf[i]
            else:
                row_copy(i).start()

        if i == 0:
            gain_load.wait()
            cw_copy.wait()
            cw_send.wait_recv()
        far = jnp.zeros((KEPT, 256), F32)
        acc = jnp.zeros((KEPT, 256), F32)
        squares = jnp.zeros((KEPT, 1), F32)
        for q in range(Z):
            wide = hbuf[i, q].astype(F32)
            squares = squares + jnp.sum(wide * wide, axis=1, keepdims=True)
            gain = gain_ref[:, pl.ds(pl.multiple_of(first_feat + q * 256, 256), 256)]
            scaled = (wide * gain).astype(BF)
            cut = slice(q * 256, (q + 1) * 256)
            far = far + jnp.dot(scaled, cw_ref[1, cut], preferred_element_type=F32)
            acc = acc + jnp.dot(scaled, cw_ref[0, cut], preferred_element_type=F32)
        ymsg[i, :, :256], ymsg[i, :, 256:] = packed(far, squares)
        ays[i] = send(ymsg.at[i], ymsg_in.at[i], ay_s.at[i], ay_r.at[i], ydev)
        own_part[i] = acc, squares

    def stage_e(i):
        ays[i].wait_recv()
        acc, squares = own_part[i]
        more, more_squares = unpacked(ymsg_in, i)
        acc = acc + more
        squares = squares + more_squares
        if i == 0:
            return acc, squares
        cmsg[i - 1, :, :256], cmsg[i - 1, :, 256:] = packed(acc, squares)
        cs[i] = send(
            cmsg.at[i - 1], crecv.at[i - 1], c_s.at[i - 1], c_r.at[i - 1], (ctx_peer(i), t)
        )
        return None

    stage_a(0)
    stage_a(1)
    diagonal = lax.broadcasted_iota(jnp.int32, (rows, rows), 0) == lax.broadcasted_iota(
        jnp.int32, (rows, rows), 1
    )
    at_row = jnp.sum(
        jnp.where(diagonal, pos_ref[...].astype(F32), 0.0), axis=1, keepdims=True
    )
    angles = at_row * freq_ref[...]
    cos_ref[...] = jnp.cos(angles)
    sin_ref[...] = jnp.sin(angles)
    stage_b(0)
    stage_a(2)
    stage_g(0)
    stage_c(0)
    stage_b(1)
    stage_a(3)
    stage_f(0)
    stage_g(1)
    stage_c(1)
    stage_b(2)
    stage_f(1)
    stage_g(2)
    stage_c(2)
    stage_b(3)
    stage_f(2)
    stage_d(0)
    stage_g(3)
    stage_d(1)
    stage_c(3)
    stage_d(2)
    stage_f(3)
    stage_e(1)
    stage_e(2)
    stage_d(3)
    stage_e(3)
    acc, squares = stage_e(0)

    @pl.when(jnp.logical_not(is_root))
    def _():
        row_copy(1).wait_recv()

    pair_copy = send(hpair.at[k], hpair.at[k], fin_s.at[0], fin_r.at[0], (sib, t))
    for i in (1, 2, 3):
        cs[i].wait_recv()
        more, more_squares = unpacked(crecv, i - 1)
        acc = acc + more
        squares = squares + more_squares
    cbuf[k] = (acc * lax.rsqrt(squares / D + EPS)).astype(BF)
    last = send(cbuf.at[k], cbuf.at[k], fin_s.at[1], fin_r.at[1], (sib, t))
    place = [place_of(kk) for kk in range(2)]
    pair_copy.wait_recv()
    for j in range(Z):
        hid_out[:, j * 256 : (j + 1) * 256] = (
            jnp.dot(place[0], hpair[0, j], preferred_element_type=F32)
            + jnp.dot(place[1], hpair[1, j], preferred_element_type=F32)
        ).astype(BF)
    last.wait_recv()
    raw = jnp.dot(place[0], cbuf[0], preferred_element_type=F32) + jnp.dot(
        place[1], cbuf[1], preferred_element_type=F32
    )
    source = lax.broadcasted_iota(jnp.int32, (HD, HD), 0)
    target = lax.broadcasted_iota(jnp.int32, (HD, HD), 1)
    swap = jnp.where(
        source == target + 1, jnp.where(target % 2 == 0, -1.0, 0.0),
        jnp.where(source == target - 1, jnp.where(target % 2 == 1, 1.0, 0.0), 0.0),
    ).astype(BF)
    key = raw[:, :HD]
    partner = jnp.dot(key.astype(BF), swap, preferred_element_type=F32)
    cache_out[:, :HD] = (key * cos_ref[...] + partner * sin_ref[...]).astype(BF)
    cache_out[:, HD:] = raw[:, HD:].astype(BF)

    for copy in pending:
        copy.wait_send()

    @pl.when(jnp.logical_not(is_root))
    def _():
        res_copy.wait_send()

    @pl.when(is_root)
    def _():
        for i in (1, 2, 3):
            row_copy(i).wait_send()

    @pl.when(is_inner)
    def _():
        for i in range(4):
            for n, j in sequence:
                piece_copy(i, j, near_dev, fw_s).wait_send()
                if n < 2:
                    cross_copy(i, j).wait_send()
                else:
                    piece_copy(i, j, cross_dev, ag_s).wait_send()

    @pl.when(is_outer)
    def _():
        for i in range(4):
            for _, j in sequence:
                out_copy(i, j).wait_send()


def fused_shards(
    residual, queries, keys_values, out_weight, norm_gain, cache_weight, positions, keep_rows, kept_count
):
    rows, width = queries.shape
    pair_first = np.arange(HD) // 2 * 2
    frequency = jnp.asarray(np.power(THETA, -pair_first / HD).astype(np.float32)[None, :])
    feat = out_weight.shape[1]
    n_ctx = D // feat
    dma = pltpu.SemaphoreType.DMA
    vmem = pl.BlockSpec(memory_space=pltpu.VMEM)
    hbm = pl.BlockSpec(memory_space=pl.ANY)
    return pl.pallas_call(
        fused_kernel,
        out_shape=(
            jax.ShapeDtypeStruct((rows, width), BF),
            jax.ShapeDtypeStruct((rows, 2 * HD), BF),
        ),
        in_specs=[hbm] * 7 + [vmem] * 3,
        out_specs=(vmem, vmem),
        scratch_shapes=[
            pltpu.VMEM((1, D), F32),
            pltpu.VMEM((1, rows), jnp.int32),
            pltpu.VMEM((rows, width), BF),
            pltpu.VMEM((rows, width), BF),
            pltpu.VMEM((n_ctx * rows, 2 * HD), BF),
            pltpu.VMEM(out_weight.shape, BF),
            pltpu.VMEM((2, feat // 2, 2 * HD), BF),
            pltpu.VMEM((2, KEPT, width + HD), BF),
            pltpu.VMEM((KEPT, width + HD), BF),
            pltpu.VMEM((2, KEPT, width), BF),
            pltpu.VMEM((KEPT, width), BF),
            pltpu.VMEM((4, KEPT, width), BF),
            pltpu.VMEM((4, KEPT, width), BF),
            pltpu.VMEM((4, Z, KEPT, 256), F32),
            pltpu.VMEM((4, Z, KEPT, 256), BF),
            pltpu.VMEM((4, Z, KEPT, 256), BF),
            pltpu.VMEM((4, Z, KEPT, 256), BF),
            pltpu.VMEM((4, Z, KEPT, 256), BF),
            pltpu.VMEM((4, Z, KEPT, 256), BF),
            pltpu.VMEM((4, Z, KEPT, 256), BF),
            pltpu.VMEM((4, KEPT, 256 + HD), BF),
            pltpu.VMEM((4, KEPT, 256 + HD), BF),
            pltpu.VMEM((3, KEPT, 256 + HD), BF),
            pltpu.VMEM((3, KEPT, 256 + HD), BF),
            pltpu.VMEM((2, KEPT, 256), BF),
            pltpu.VMEM((2, Z, KEPT, 256), BF),
            pltpu.VMEM((rows, HD), F32),
            pltpu.VMEM((rows, HD), F32),
            dma((7,)), dma((3,)), dma((3,)), dma((2,)), dma((2,)), dma, dma((4,)),
            dma((3,)), dma((3,)), dma((4, 4)), dma((4, 4)), dma((4, 4)), dma((4, 4)), dma((4, 4)),
            dma((4, 4)), dma((4, 4)), dma((4, 4)), dma((4,)), dma((4,)), dma, dma, dma((3,)), dma((3,)),
            dma((4,)), dma, dma((2,)), dma((2,)),
        ],
        compiler_params=pltpu.CompilerParams(
            collective_id=0, has_side_effects=True, vmem_limit_bytes=60 * 1024 * 1024
        ),
        cost_estimate=pl.CostEstimate(flops=6_000_000_000, bytes_accessed=8_000_000, transcendentals=1_400_000),
    )(
        queries, residual, keys_values, out_weight, cache_weight,
        norm_gain[None, :], keep_rows[None, :], kept_count[None, :],
        positions[None, :], frequency,
    )


def solution(mesh):
    in_specs = (
        P("ctx", "tp"),
        P("ctx", "tp"),
        P("ctx", None),
        P("tp", "ctx"),
        P(),
        P(None, "tp"),
        P("ctx"),
        P("ctx"),
        P("ctx"),
    )
    out_specs = (P("ctx", "tp"), P("ctx", "tp"))
    fits = mesh.shape["ctx"] == 4 and mesh.shape["tp"] == 8
    body = fused_shards if fits else shards
    return jax.shard_map(body, mesh=mesh, in_specs=in_specs, out_specs=out_specs, check_vma=False)
```

```python
import math

import jax
import numpy as np
import jax.numpy as jnp
from jax import lax
from jax.experimental import pallas as pl
from jax.experimental.pallas import tpu as pltpu
from jax.sharding import PartitionSpec as P

D = 8192
HQ = 64
KVH = 8
HD = 128


THETA = 1000000.0
EPS = 1e-06


def rotate_pairs(cache_rows, position_ids, first_col, head_dim):
    pair_count = cache_rows.shape[1] // 2
    columns = first_col + 2 * jnp.arange(pair_count, dtype=jnp.int32)
    within = columns % (2 * head_dim)
    is_key = within < head_dim
    exponent = jnp.where(is_key, within, 0).astype(jnp.float32) / head_dim
    frequency = jnp.power(jnp.float32(THETA), -exponent)
    angles = position_ids.astype(jnp.float32)[:, None] * frequency[None, :]
    paired = cache_rows.reshape(cache_rows.shape[0], pair_count, 2)
    first_half = paired[..., 0]
    second = paired[..., 1]
    cosine = jnp.cos(angles)
    sine_rows = jnp.sin(angles)
    turned_first = first_half * cosine - second * sine_rows
    turned_second = second * cosine + first_half * sine_rows
    turned = jnp.stack(
        [jnp.where(is_key, turned_first, first_half), jnp.where(is_key, turned_second, second)], -1
    )
    return turned.reshape(cache_rows.shape)


def shards(
    residual,
    queries,
    keys_values,
    out_weight,
    norm_gain,
    cache_weight,
    positions,
    keep_rows,
    kept_count,
):
    row_count = residual.shape[0]
    ctx_index = lax.axis_index("ctx")
    tp_index = lax.axis_index("tp")
    head_count = queries.shape[1] // HD
    kv_head = tp_index * head_count // (HQ // KVH)
    head_block = lax.dynamic_slice_in_dim(keys_values, kv_head * 2 * HD, 2 * HD, 1)
    key_rows = head_block[:, :HD]
    value_rows = head_block[:, HD:]
    query_rows = queries.reshape(row_count, head_count, HD)
    own_index = ctx_index * row_count + jnp.arange(row_count, dtype=jnp.int32)
    score_scale = 1.0 / math.sqrt(HD)
    running_max = jnp.full((row_count, head_count), -1e30, jnp.float32)
    key_block = lax.all_gather(key_rows, "ctx", axis=0, tiled=True)
    value_block = lax.all_gather(value_rows, "ctx", axis=0, tiled=True)
    block_rows = key_block.shape[0]
    scores = (
        jnp.einsum("rgd,kd->rgk", query_rows, key_block, preferred_element_type=jnp.float32)
        * score_scale
    )
    visible = jnp.arange(block_rows, dtype=jnp.int32)[None, :] <= own_index[:, None]
    visible = visible[:, None, :]
    scores = jnp.where(visible, scores, -1e30)
    new_max = jnp.maximum(running_max, jnp.max(scores, axis=-1))
    weights = jnp.where(visible, jnp.exp(scores - new_max[..., None]), 0.0)
    new_sum = jnp.sum(weights, axis=-1)
    update = jnp.einsum(
        "rgk,kd->rgd", weights.astype(jnp.bfloat16), value_block, preferred_element_type=jnp.float32
    )
    attended = (
        (update / new_sum[..., None]).reshape(row_count, head_count * HD).astype(jnp.bfloat16)
    )
    own_count = kept_count[0]
    valid_rows = jnp.arange(row_count, dtype=jnp.int32) < own_count
    partials = jnp.dot(
        attended,
        lax.all_gather(out_weight, "ctx", axis=1, tiled=True),
        preferred_element_type=jnp.float32,
    )
    group_sums = lax.psum_scatter(
        partials.astype(jnp.bfloat16), "tp", scatter_dimension=1, tiled=True
    ).astype(jnp.float32)
    hidden = (residual.astype(jnp.float32) + group_sums).astype(jnp.bfloat16)
    feat_width = hidden.shape[1]
    wide_hidden = hidden.astype(jnp.float32)
    square_total = lax.psum(jnp.sum(wide_hidden * wide_hidden, axis=-1), "tp")
    inverse = lax.rsqrt(square_total / D + EPS)
    gain_part = lax.dynamic_slice_in_dim(norm_gain, tp_index * feat_width, feat_width)
    normed = (wide_hidden * inverse[:, None] * gain_part[None, :]).astype(jnp.bfloat16)
    gathered = lax.all_gather(normed, "tp", axis=1, tiled=True)
    cache_rows = jnp.dot(gathered, cache_weight, preferred_element_type=jnp.float32)
    cache_rot = rotate_pairs(cache_rows, positions, tp_index * cache_rows.shape[1], HD).astype(
        jnp.bfloat16
    )
    kept_flags = jnp.zeros((row_count,), jnp.int32).at[keep_rows].set(valid_rows.astype(jnp.int32))
    kept_mask = kept_flags[:, None] > 0
    kept_hidden = jnp.where(kept_mask, hidden, jnp.zeros_like(hidden))
    kept_cache = jnp.where(kept_mask, cache_rot, jnp.zeros_like(cache_rot))
    return (kept_hidden, kept_cache)


KEPT = 160
Z = 4
MESH = pl.DeviceIdType.MESH
BF = jnp.bfloat16
F32 = jnp.float32


def fused_kernel(
    q_hbm, r_hbm, kv_hbm, w_hbm, cw_hbm, gain_hbm, keep_hbm, count_ref, pos_ref, freq_ref,
    hid_out, cache_out,
    gain_ref, keep_ref, q_ref, r_ref, kvbuf, w_ref, cw_ref, qown, qrecv, rown, rrecv, resbuf, attb, ownp, ysend, yrecv,
    zsum, zrecv, xrecv, hbuf, ymsg, ymsg_in, cmsg, crecv, cbuf, hpair, cos_ref, sin_ref,
    loc_sem, kv_s, kv_r, q_s, q_r, res_s, res_r, att_s, att_r, y_s, y_r, z_s, z_r, x_r,
    ag_s, ag_r, fw_s, ay_s, ay_r, cw_s, cw_r, c_s, c_r, row_s, row_r, fin_s, fin_r,
):
    c = lax.axis_index("ctx")
    t = lax.axis_index("tp")
    p, k = c // 2, c % 2
    z, y = t // 2, t % 2
    rows = q_ref.shape[0]
    near = z + 1 - 2 * (z % 2)
    cross = Z - 1 - z
    is_inner = (z + 1) // 2 == 1

    def ctx_peer(i):
        return ((p + i // 2) % 2) * 2 + (k + i % 2) % 2

    sib = ctx_peer(1)
    ydev = (c, 2 * z + 1 - y)
    is_root = c == z
    pending = []

    def remote(src, dst, ss, rs, dev):
        return pltpu.make_async_remote_copy(
            src_ref=src, dst_ref=dst, send_sem=ss, recv_sem=rs, device_id=dev, device_id_type=MESH
        )

    def send(src, dst, ss, rs, dev):
        copy = remote(src, dst, ss, rs, dev)
        copy.start()
        pending.append(copy)
        return copy

    feat = cw_ref.shape[1]
    own_kv = kvbuf.at[pl.ds(pl.multiple_of(c * rows, rows), rows)]
    kv_copy = pltpu.make_async_copy(
        kv_hbm.at[:, pl.ds(pl.multiple_of(t * 2 * HD, 2 * HD), 2 * HD)], own_kv, loc_sem.at[2]
    )
    kv_copy.start()
    keep_load = pltpu.make_async_copy(keep_hbm, keep_ref, loc_sem.at[5])
    keep_load.start()
    q_load = pltpu.make_async_copy(q_hbm, q_ref, loc_sem.at[3])
    q_load.start()
    r_load = pltpu.make_async_copy(r_hbm, r_ref, loc_sem.at[4])
    r_load.start()
    w_copy = pltpu.make_async_copy(w_hbm, w_ref, loc_sem.at[0])
    w_copy.start()
    first_feat = pl.multiple_of((2 * c + y) * feat, feat)
    cw_copy = pltpu.make_async_copy(cw_hbm.at[pl.ds(first_feat, feat)], cw_ref.at[0], loc_sem.at[1])
    cw_copy.start()

    gain_load = pltpu.make_async_copy(gain_hbm, gain_ref, loc_sem.at[6])
    gain_load.start()

    barrier = pltpu.get_barrier_semaphore()
    partners = [(ctx_peer(i), t) for i in (1, 2, 3)]
    partners += [(c, zz * 2 + y) for zz in (near, cross)] + [ydev]
    for dev in partners:
        pl.semaphore_signal(barrier, inc=1, device_id=dev, device_id_type=MESH)
    pl.semaphore_wait(barrier, len(partners))

    count = count_ref[...]
    keep_load.wait()
    base = jnp.where(k == 0, 0, 2 * KEPT - count)
    chosen = keep_ref[...] == lax.broadcasted_iota(jnp.int32, (rows, rows), 0)
    rank = lax.broadcasted_iota(jnp.int32, (rows, KEPT), 0)
    slot_at = lax.broadcasted_iota(jnp.int32, (rows, KEPT), 1)
    chosen = jnp.where(chosen, 1.0, 0.0).astype(BF)

    def place_of(kk):
        hit = (rank + base == slot_at + kk * KEPT) & (rank < count)
        return jnp.dot(
            chosen, jnp.where(hit, 1.0, 0.0).astype(BF), preferred_element_type=F32
        ).astype(BF)

    place_sib = place_of(1 - k)
    place_own = place_of(k)
    row_id = lax.broadcasted_iota(jnp.int32, (rows, HD), 0).astype(F32)
    lane = lax.broadcasted_iota(jnp.int32, (rows, HD), 1)
    tags = jnp.where(lane == 0, row_id, jnp.where(lane == 1, 1.0, 0.0)).astype(BF)
    width = q_ref.shape[1]

    def pick(sel, what):
        return lax.dot_general(
            sel, what, (((0,), (0,)), ((), ())), preferred_element_type=F32
        ).astype(BF)

    kv_copy.wait()
    kv_far = send(own_kv, own_kv, kv_s.at[0], kv_r.at[0], (ctx_peer(2), t))
    kv_sib = send(own_kv, own_kv, kv_s.at[1], kv_r.at[1], (sib, t))
    cw_send = send(
        cw_hbm.at[pl.ds(pl.multiple_of((2 * c + 1 - y) * feat, feat), feat)],
        cw_ref.at[1], cw_s, cw_r, ydev,
    )
    q_load.wait()
    qown[0, :, :width] = pick(place_sib, q_ref[...])
    qown[0, :, width:] = pick(place_sib, tags)
    q_copy = send(qown.at[0], qrecv, q_s.at[0], q_r.at[0], (sib, t))
    r_load.wait()
    rown[0] = pick(place_sib, r_ref[...])
    r_copy = send(rown.at[0], rrecv, q_s.at[1], q_r.at[1], (sib, t))
    qown[1, :, :width] = pick(place_own, q_ref[...])
    qown[1, :, width:] = pick(place_own, tags)
    rown[1] = pick(place_own, r_ref[...])

    kv_far.wait_recv()
    far_kv = kvbuf.at[pl.ds(pl.multiple_of(ctx_peer(2) * rows, rows), rows)]
    kv_diag = send(far_kv, far_kv, kv_s.at[2], kv_r.at[2], (sib, t))
    q_copy.wait_recv()
    own_tag = qown[1, :, width:].astype(F32)
    sib_tag = qrecv[:, width:].astype(F32)
    first_own = (c * rows).astype(F32)
    first_sib = (sib * rows).astype(F32)
    limit = (
        own_tag[:, 0:1] + first_own * own_tag[:, 1:2] + sib_tag[:, 0:1] + first_sib * sib_tag[:, 1:2]
    )
    qown[1, :, :width] = qown[1, :, :width] + qrecv[:, :width]

    r_copy.wait_recv()
    rown[1] = rown[1] + rrecv[...]
    res_slot = ((p + z // 2) % 2) * 2 + (k + z) % 2
    res_copy = remote(
        rown.at[1], resbuf.at[res_slot], res_s, res_r.at[res_slot], (z, t)
    )

    @pl.when(is_root)
    def _():
        resbuf[0] = rown[1]

    @pl.when(jnp.logical_not(is_root))
    def _():
        res_copy.start()

    kv_sib.wait_recv()
    kv_diag.wait_recv()
    total = kvbuf.shape[0]
    col_id = lax.broadcasted_iota(jnp.int32, (KEPT, total), 1).astype(F32)
    group = 4
    seen = col_id <= limit
    seen = jnp.concatenate([seen] * group, axis=0)
    scale = math.log2(math.e) / math.sqrt(HD)
    keys = kvbuf[:, :HD]
    values = kvbuf[:, HD:]
    for first in range(0, width // HD, group):
        heads = [slice(h * HD, (h + 1) * HD) for h in range(first, first + group)]
        s = lax.dot_general(
            jnp.concatenate([qown[1, :, cols] for cols in heads], axis=0),
            keys,
            (((1,), (1,)), ((), ())),
            preferred_element_type=F32,
        )
        s = jnp.where(seen, s, -1e30)
        top = jnp.max(s, axis=1, keepdims=True)
        e = jnp.exp2((s - top) * scale)
        den = jnp.sum(e, axis=1, keepdims=True)
        mixed = jnp.dot(e.astype(BF), values, preferred_element_type=F32) / den
        for n, cols in enumerate(heads):
            attb[0, :, cols] = mixed[n * KEPT : (n + 1) * KEPT].astype(BF)

    att_cp = send(attb.at[0], attb.at[2], att_s.at[0], att_r.at[0], (ctx_peer(2), t))
    att_sib = send(attb.at[0], attb.at[1], att_s.at[1], att_r.at[1], (sib, t))
    half = Z * 256
    other = 2 * (1 - z // 2)
    mine = 2 - other
    is_outer = jnp.logical_not(is_inner)
    near_dev = (c, near * 2 + y)
    cross_dev = (c, cross * 2 + y)
    sequence = [(jj, other + jj) for jj in range(2)] + [(2 + jj, mine + jj) for jj in range(2)]

    def piece_of(who, j):
        return pl.ds(pl.multiple_of(who * half + j * 256, 256), 256)

    def y_copy(i, j):
        return remote(ysend.at[i, j], yrecv.at[i, j], y_s.at[i, j], y_r.at[i, j], ydev)

    def out_copy(i, j):
        return remote(zsum.at[i, j], zrecv.at[i, j], z_s.at[i, j], z_r.at[i, j], near_dev)

    def cross_copy(i, j):
        return remote(zsum.at[i, j], xrecv.at[i, j], z_s.at[i, j], x_r.at[i, j], cross_dev)
    w_copy.wait()
    fwd = {}
    ays, cs = {}, {}

    def stage_a(i):
        if i == 1:
            att_sib.wait_recv()
        if i == 2:
            att_cp.wait_recv()
            fwd[0] = send(attb.at[2], attb.at[3], att_s.at[2], att_r.at[2], (sib, t))
        if i == 3:
            fwd[0].wait_recv()
        for _, j in sequence:
            ysend[i, j] = jnp.dot(
                attb[i], w_ref[:, piece_of(1 - y, j)], preferred_element_type=F32
            ).astype(BF)
            copy = y_copy(i, j)
            copy.start()
            pending.append(copy)
        for _, j in sequence:
            ownp[i, j] = jnp.dot(
                attb[i], w_ref[:, piece_of(y, j)], preferred_element_type=F32
            )

    def stage_b(i):
        @pl.when(is_root)
        def _():
            if i > 0:
                remote(
                    rown.at[1], resbuf.at[i], res_s, res_r.at[i], (ctx_peer(i), t)
                ).wait_recv()
            for j in range(Z):
                ownp[i, j] = ownp[i, j] + resbuf[i, :, j * 256 : (j + 1) * 256].astype(F32)

        for _, j in sequence:
            y_copy(i, j).wait_recv()
            total = ownp[i, j] + yrecv[i, j].astype(F32)

            @pl.when(is_outer)
            def _():
                zsum[i, j] = total.astype(BF)
                out_copy(i, j).start()

            @pl.when(is_inner)
            def _():
                ownp[i, j] = total

    def stage_g(i):
        @pl.when(is_inner)
        def _():
            for n, j in sequence:
                out_copy(i, j).wait_recv()
                total = ownp[i, j] + zrecv[i, j].astype(F32)
                if n < 2:
                    zsum[i, j] = total.astype(BF)
                    cross_copy(i, j).start()
                else:
                    ownp[i, j] = total

    def piece_copy(i, j, dev, sem):
        piece = hbuf.at[i, j]
        return remote(piece, piece, sem.at[i, j], ag_r.at[i, j], dev)

    def stage_c(i):
        @pl.when(is_inner)
        def _():
            for n, j in sequence[2:]:
                cross_copy(i, j).wait_recv()
                hbuf[i, j] = (ownp[i, j] + xrecv[i, j].astype(F32)).astype(BF)
                piece_copy(i, j, cross_dev, ag_s).start()
                piece_copy(i, j, near_dev, fw_s).start()

    def stage_f(i):
        @pl.when(is_inner)
        def _():
            for n, j in sequence[:2]:
                piece_copy(i, j, cross_dev, ag_s).wait_recv()
                piece_copy(i, j, near_dev, fw_s).start()

    def row_copy(i):
        return remote(
            hbuf.at[i], hpair.at[(k + i % 2) % 2], row_s.at[i], row_r, (ctx_peer(i), t)
        )

    own_part = {}

    def packed(acc, squares):
        coarse = squares.astype(BF).astype(F32)
        at = lax.broadcasted_iota(jnp.int32, (KEPT, HD), 1)
        tail = jnp.where(at == 0, coarse, jnp.where(at == 1, squares - coarse, 0.0))
        return acc.astype(BF), tail.astype(BF)

    def unpacked(ref, i):
        tail = ref[i, :, 256:].astype(F32)
        return ref[i, :, :256].astype(F32), tail[:, 0:1] + tail[:, 1:2]

    def stage_d(i):
        @pl.when(is_outer)
        def _():
            for _, j in sequence[2:] + sequence[:2]:
                piece_copy(i, j, near_dev, fw_s).wait_recv()

        @pl.when(is_root)
        def _():
            if i == 0:
                hpair[k] = hbuf[i]
            else:
                row_copy(i).start()

        if i == 0:
            gain_load.wait()
            cw_copy.wait()
            cw_send.wait_recv()
        far = jnp.zeros((KEPT, 256), F32)
        acc = jnp.zeros((KEPT, 256), F32)
        squares = jnp.zeros((KEPT, 1), F32)
        parts = []
        for q in range(Z):
            wide = hbuf[i, q].astype(F32)
            squares = squares + jnp.sum(wide * wide, axis=1, keepdims=True)
            gain = gain_ref[:, pl.ds(pl.multiple_of(first_feat + q * 256, 256), 256)]
            scaled = (wide * gain).astype(BF)
            cut = slice(q * 256, (q + 1) * 256)
            parts.append((scaled, cut))
            far = far + jnp.dot(scaled, cw_ref[1, cut], preferred_element_type=F32)
        ymsg[i, :, :256], ymsg[i, :, 256:] = packed(far, squares)
        ays[i] = send(ymsg.at[i], ymsg_in.at[i], ay_s.at[i], ay_r.at[i], ydev)
        for scaled, cut in parts:
            acc = acc + jnp.dot(scaled, cw_ref[0, cut], preferred_element_type=F32)
        own_part[i] = acc, squares

    def stage_e(i):
        ays[i].wait_recv()
        acc, squares = own_part[i]
        more, more_squares = unpacked(ymsg_in, i)
        acc = acc + more
        squares = squares + more_squares
        if i == 0:
            return acc, squares
        cmsg[i - 1, :, :256], cmsg[i - 1, :, 256:] = packed(acc, squares)
        cs[i] = send(
            cmsg.at[i - 1], crecv.at[i - 1], c_s.at[i - 1], c_r.at[i - 1], (ctx_peer(i), t)
        )
        return None

    stage_a(0)
    stage_a(1)
    diagonal = lax.broadcasted_iota(jnp.int32, (rows, rows), 0) == lax.broadcasted_iota(
        jnp.int32, (rows, rows), 1
    )
    at_row = jnp.sum(
        jnp.where(diagonal, pos_ref[...].astype(F32), 0.0), axis=1, keepdims=True
    )
    angles = at_row * freq_ref[...]
    cos_ref[...] = jnp.cos(angles)
    sin_ref[...] = jnp.sin(angles)
    stage_b(0)
    stage_a(2)
    stage_g(0)
    stage_c(0)
    stage_b(1)
    stage_a(3)
    stage_f(0)
    stage_g(1)
    stage_d(0)
    stage_c(1)
    stage_b(2)
    stage_f(1)
    stage_g(2)
    stage_d(1)
    stage_c(2)
    stage_b(3)
    stage_f(2)
    stage_g(3)
    stage_e(1)
    stage_d(2)
    stage_c(3)
    stage_f(3)
    stage_e(2)
    stage_d(3)

    stage_e(3)
    acc, squares = stage_e(0)

    @pl.when(jnp.logical_not(is_root))
    def _():
        row_copy(1).wait_recv()

    pair_copy = send(hpair.at[k], hpair.at[k], fin_s.at[0], fin_r.at[0], (sib, t))
    for i in (1, 2, 3):
        cs[i].wait_recv()
        more, more_squares = unpacked(crecv, i - 1)
        acc = acc + more
        squares = squares + more_squares
    cbuf[k] = (acc * lax.rsqrt(squares / D + EPS)).astype(BF)
    last = send(cbuf.at[k], cbuf.at[k], fin_s.at[1], fin_r.at[1], (sib, t))
    place = [place_of(kk) for kk in range(2)]
    pair_copy.wait_recv()
    for j in range(Z):
        hid_out[:, j * 256 : (j + 1) * 256] = (
            jnp.dot(place[0], hpair[0, j], preferred_element_type=F32)
            + jnp.dot(place[1], hpair[1, j], preferred_element_type=F32)
        ).astype(BF)
    last.wait_recv()
    raw = jnp.dot(place[0], cbuf[0], preferred_element_type=F32) + jnp.dot(
        place[1], cbuf[1], preferred_element_type=F32
    )
    source = lax.broadcasted_iota(jnp.int32, (HD, HD), 0)
    target = lax.broadcasted_iota(jnp.int32, (HD, HD), 1)
    swap = jnp.where(
        source == target + 1, jnp.where(target % 2 == 0, -1.0, 0.0),
        jnp.where(source == target - 1, jnp.where(target % 2 == 1, 1.0, 0.0), 0.0),
    ).astype(BF)
    key = raw[:, :HD]
    partner = jnp.dot(key.astype(BF), swap, preferred_element_type=F32)
    cache_out[:, :HD] = (key * cos_ref[...] + partner * sin_ref[...]).astype(BF)
    cache_out[:, HD:] = raw[:, HD:].astype(BF)

    for copy in pending:
        copy.wait_send()

    @pl.when(jnp.logical_not(is_root))
    def _():
        res_copy.wait_send()

    @pl.when(is_root)
    def _():
        for i in (1, 2, 3):
            row_copy(i).wait_send()

    @pl.when(is_inner)
    def _():
        for i in range(4):
            for n, j in sequence:
                piece_copy(i, j, near_dev, fw_s).wait_send()
                if n < 2:
                    cross_copy(i, j).wait_send()
                else:
                    piece_copy(i, j, cross_dev, ag_s).wait_send()

    @pl.when(is_outer)
    def _():
        for i in range(4):
            for _, j in sequence:
                out_copy(i, j).wait_send()


def fused_shards(
    residual, queries, keys_values, out_weight, norm_gain, cache_weight, positions, keep_rows, kept_count
):
    rows, width = queries.shape
    pair_first = np.arange(HD) // 2 * 2
    frequency = jnp.asarray(np.power(THETA, -pair_first / HD).astype(np.float32)[None, :])
    feat = out_weight.shape[1]
    n_ctx = D // feat
    dma = pltpu.SemaphoreType.DMA
    vmem = pl.BlockSpec(memory_space=pltpu.VMEM)
    hbm = pl.BlockSpec(memory_space=pl.ANY)
    return pl.pallas_call(
        fused_kernel,
        out_shape=(
            jax.ShapeDtypeStruct((rows, width), BF),
            jax.ShapeDtypeStruct((rows, 2 * HD), BF),
        ),
        in_specs=[hbm] * 7 + [vmem] * 3,
        out_specs=(vmem, vmem),
        scratch_shapes=[
            pltpu.VMEM((1, D), F32),
            pltpu.VMEM((1, rows), jnp.int32),
            pltpu.VMEM((rows, width), BF),
            pltpu.VMEM((rows, width), BF),
            pltpu.VMEM((n_ctx * rows, 2 * HD), BF),
            pltpu.VMEM(out_weight.shape, BF),
            pltpu.VMEM((2, feat // 2, 2 * HD), BF),
            pltpu.VMEM((2, KEPT, width + HD), BF),
            pltpu.VMEM((KEPT, width + HD), BF),
            pltpu.VMEM((2, KEPT, width), BF),
            pltpu.VMEM((KEPT, width), BF),
            pltpu.VMEM((4, KEPT, width), BF),
            pltpu.VMEM((4, KEPT, width), BF),
            pltpu.VMEM((4, Z, KEPT, 256), F32),
            pltpu.VMEM((4, Z, KEPT, 256), BF),
            pltpu.VMEM((4, Z, KEPT, 256), BF),
            pltpu.VMEM((4, Z, KEPT, 256), BF),
            pltpu.VMEM((4, Z, KEPT, 256), BF),
            pltpu.VMEM((4, Z, KEPT, 256), BF),
            pltpu.VMEM((4, Z, KEPT, 256), BF),
            pltpu.VMEM((4, KEPT, 256 + HD), BF),
            pltpu.VMEM((4, KEPT, 256 + HD), BF),
            pltpu.VMEM((3, KEPT, 256 + HD), BF),
            pltpu.VMEM((3, KEPT, 256 + HD), BF),
            pltpu.VMEM((2, KEPT, 256), BF),
            pltpu.VMEM((2, Z, KEPT, 256), BF),
            pltpu.VMEM((rows, HD), F32),
            pltpu.VMEM((rows, HD), F32),
            dma((7,)), dma((3,)), dma((3,)), dma((2,)), dma((2,)), dma, dma((4,)),
            dma((3,)), dma((3,)), dma((4, 4)), dma((4, 4)), dma((4, 4)), dma((4, 4)), dma((4, 4)),
            dma((4, 4)), dma((4, 4)), dma((4, 4)), dma((4,)), dma((4,)), dma, dma, dma((3,)), dma((3,)),
            dma((4,)), dma, dma((2,)), dma((2,)),
        ],
        compiler_params=pltpu.CompilerParams(
            collective_id=0, has_side_effects=True, vmem_limit_bytes=60 * 1024 * 1024
        ),
        cost_estimate=pl.CostEstimate(flops=6_000_000_000, bytes_accessed=8_000_000, transcendentals=1_400_000),
    )(
        queries, residual, keys_values, out_weight, cache_weight,
        norm_gain[None, :], keep_rows[None, :], kept_count[None, :],
        positions[None, :], frequency,
    )


def solution(mesh):
    in_specs = (
        P("ctx", "tp"),
        P("ctx", "tp"),
        P("ctx", None),
        P("tp", "ctx"),
        P(),
        P(None, "tp"),
        P("ctx"),
        P("ctx"),
        P("ctx"),
    )
    out_specs = (P("ctx", "tp"), P("ctx", "tp"))
    fits = mesh.shape["ctx"] == 4 and mesh.shape["tp"] == 8
    body = fused_shards if fits else shards
    return jax.shard_map(body, mesh=mesh, in_specs=in_specs, out_specs=out_specs, check_vma=False)
```
